32 devices in a mesh: grp: 2 (over x), kv: 16 (over z, y, core).
Axes of the slice: x: 2, y: 2, z: 4, core: 2. Of those that a mesh axis runs over, the one named last changes fastest.
Arguments:
- queries: bfloat16 [8192, 640], P(('grp', 'kv')), parts along dimension 0, may hold values from -150 to 150
- ext_kv: bfloat16 [8192, 256], P(('grp', 'kv')), parts along dimension 0, may hold values from -6 to 6
- page_store: bfloat16 [64, 128, 1024], P(('grp', 'kv')), parts along dimension 0, may hold values from -6 to 6
- prefix_hidden: bfloat16 [32, 128, 5120], P(('grp', 'kv')), parts along dimension 0, may hold values from -6 to 6
- kv_weight: bfloat16 [5120, 1024], P('kv'), may hold values from -0.078125 to 0.078125
- kv_bias: bfloat16 [1024], replicated, may hold values from -3 to 3
- reuse: int32 [56, 3], P('grp'), parts along dimension 0, may hold values from 0 to 31, as said below
Outputs:
- attended: bfloat16 [8192, 640], P(('grp', 'kv')), parts along dimension 0
The draws below stay inside these ranges and needn't reach their ends.
There are 2 independent parts, one for each index of `grp`. The reference program is written for one: setup_inputs(seed, part) draws one part's arguments, and reference() takes and returns one part's arrays. A program takes and returns all parts, laid end to end along the dimension named above; an argument that names none is the same for every part. Nothing has to cross between parts.
Inputs may be any that keep to these rules, and one draw needn't show every extreme that they name: `reuse`: row p describes prefix page p. Column 0 is 1 if the page is cached, else 0. For a cached page column 1 is the store slot holding it (device d holds store slots 2 * d to 2 * d + 1); for the others column 2 is the recompute slot whose hidden rows give it (device d holds recompute slot d). The other column of a row is a valid index with no meaning. No store slot and no recompute slot serves two pages. Every device holds at most 2 pages of the prefix in its store and recompute slots together, and some devices hold exactly 2.
All inputs are finite; a program needn't handle non-finite values.
Results may differ from the reference program's by a relative error of at most 0.012.
Values may be sent and summed in bfloat16 or wider, within the bound.
No kernel may reach another device: no remote copies, remote signals or barrier semaphores. Data moves between devices by JAX's collectives and lax.ppermute only.
A program may use at most 128 MiB of HBM per device.

```python
import math
import jax
import jax.numpy as jnp
from jax import lax

D = 5120
KV_HEADS = 4
GQ = 5
HEAD_DIM = 128
PAGE = 128
SLOTS = 2
LIVE_DEV = 2
KV_DEVS = 16
EXT = 1024
PAGES = 28
STORE = 32
PREFIX = 3584


def draw_reuse(key, part):
    key = jax.random.fold_in(key, 17)
    key_keep, key_order, key_pages, key_store, key_fresh = jax.random.split(key, 5)
    slot_kinds = SLOTS + 1
    tickets = jax.random.permutation(key_keep, LIVE_DEV * KV_DEVS)
    keep_flags = jnp.zeros((LIVE_DEV * KV_DEVS,), jnp.int32).at[tickets[:PAGES]].set(1)
    live_counts = keep_flags.reshape(KV_DEVS, LIVE_DEV).sum(axis=1)
    order_scores = jax.random.randint(key_order, (KV_DEVS, slot_kinds), 0, 1 << 20) * 8 + jnp.arange(slot_kinds, dtype=jnp.int32)[None, :]
    slot_ranks = jnp.argsort(jnp.argsort(order_scores, axis=1), axis=1)
    live_slots = (slot_ranks < live_counts[:, None]).reshape(-1)
    flat_index = jnp.arange(slot_kinds * KV_DEVS, dtype=jnp.int32)
    owner_device = flat_index // slot_kinds
    slot_kind = flat_index % slot_kinds
    shuffle_scores = jax.random.randint(key_pages, (slot_kinds * KV_DEVS,), 0, 1 << 16) * (8 * KV_DEVS) + flat_index
    shuffle_scores = jnp.where(live_slots, shuffle_scores, (1 << 30) + flat_index)
    chosen = jnp.argsort(shuffle_scores)[:PAGES]
    is_store = slot_kind[chosen] < SLOTS
    store_slot = owner_device[chosen] * SLOTS + jnp.minimum(slot_kind[chosen], SLOTS - 1)
    fresh_slot = owner_device[chosen]
    junk_store = jax.random.randint(key_store, (PAGES,), 0, SLOTS * KV_DEVS)
    junk_fresh = jax.random.randint(key_fresh, (PAGES,), 0, KV_DEVS)
    cached_flag = is_store.astype(jnp.int32)
    store_column = jnp.where(is_store, store_slot, junk_store)
    fresh_column = jnp.where(is_store, junk_fresh, fresh_slot)
    return jnp.stack([cached_flag, store_column, fresh_column], axis=1).astype(jnp.int32)


def draw_queries(key, part):
    key = jax.random.fold_in(key, 29)
    key_values = jax.random.fold_in(key, 0)
    row_total = KV_HEADS * EXT
    row_width = GQ * HEAD_DIM
    values = 3.0 * jax.random.truncated_normal(key_values, -6.0, 6.0, (row_total, row_width), jnp.float32)
    return values.astype(jnp.bfloat16)


def shard_levels(own_key, dims, cuts, smallest, top_value):
    def one(dim, blocks):
        draws = jax.random.uniform(jax.random.fold_in(jax.random.fold_in(own_key, 6), dim), (blocks,), jnp.float32, smallest / len(cuts), top_value / len(cuts))
        return jnp.repeat(jnp.exp(draws), dims[dim] // blocks).reshape((-1,) + (1,) * (len(dims) - dim - 1))

    level = one(*cuts[0])
    for cut in cuts[1:]:
        level = level * one(*cut)
    return level


def normal_values(stream_key, dims, spread, reach, cuts=(), kind=jnp.bfloat16):
    loudness = shard_levels(stream_key, dims, cuts, -0.22, 0.18) if cuts else 1.0
    values = jax.random.normal(stream_key, dims, jnp.float32) * spread * loudness
    return jnp.minimum(jnp.maximum(values, -reach), reach).astype(kind)


def setup_inputs(seed: int = 0, part: int = 0) -> dict:
    streams_of = jax.random.split(jax.random.key(seed), 8)
    part_keys = jax.random.split(jax.random.fold_in(streams_of[7], part), 8)
    return {
        "queries": draw_queries(jax.random.fold_in(jax.random.fold_in(streams_of[7], part), 71), part),
        "ext_kv": normal_values(part_keys[1], (KV_HEADS * EXT, 2 * HEAD_DIM), 1.0, 6.0, ((0, 16),)),
        "page_store": normal_values(part_keys[2], (STORE, PAGE, 2 * KV_HEADS * HEAD_DIM), 1.0, 6.0, ((0, 16),)),
        "prefix_hidden": normal_values(part_keys[3], (KV_DEVS, PAGE, D), 1.0, 6.0, ((0, 16),)),
        "kv_weight": normal_values(streams_of[4], (D, 2 * KV_HEADS * HEAD_DIM), D ** -0.5, 0.078125, ((0, 16),)),
        "kv_bias": normal_values(streams_of[5], (2 * KV_HEADS * HEAD_DIM,), 0.5, 3.0),
        "reuse": draw_reuse(jax.random.fold_in(jax.random.fold_in(streams_of[7], part), 71), part),
    }


ROPE_BASE = 1000000.0
MASK_VALUE = -1e30


def rotate(vectors, positions):
    half_dim = vectors.shape[-1] // 2
    frequency = ROPE_BASE ** (-jnp.arange(half_dim, dtype=jnp.float32) * 2.0 / vectors.shape[-1])
    angles = positions.astype(jnp.float32)[:, None] * frequency[None, :]
    cosine = jnp.cos(angles)[:, None, :]
    sine_part = jnp.sin(angles)[:, None, :]
    leading = vectors[..., :half_dim]
    trailing = vectors[..., half_dim:]
    return jnp.concatenate([leading * cosine - trailing * sine_part, trailing * cosine + leading * sine_part], axis=-1)


def recompute_page(hidden_rows, kv_weight, kv_bias, page_index):
    projected = jnp.dot(hidden_rows, kv_weight, preferred_element_type=jnp.float32) + kv_bias.astype(jnp.float32)
    projected = projected.reshape(PAGE, KV_HEADS, 2, HEAD_DIM)
    positions = page_index * PAGE + jnp.arange(PAGE, dtype=jnp.int32)
    rotated_keys = rotate(projected[:, :, 0, :], positions)
    joined = jnp.stack([rotated_keys, projected[:, :, 1, :]], axis=2)
    return joined.reshape(PAGE, KV_HEADS * 2 * HEAD_DIM).astype(jnp.bfloat16)


def reference(queries, ext_kv, page_store, prefix_hidden, kv_weight, kv_bias, reuse):
    cached = reuse[:, 0] == 1
    fresh_match = jnp.logical_not(cached)[:, None] & (reuse[:, 2][:, None] == jnp.arange(KV_DEVS, dtype=jnp.int32)[None, :])
    fresh_page = jnp.sum(jnp.where(fresh_match, jnp.arange(PAGES, dtype=jnp.int32)[:, None], 0), axis=0).astype(jnp.int32)

    def project_slot(slot_pair):
        return recompute_page(slot_pair[0], kv_weight, kv_bias, slot_pair[1])

    recomputed = lax.map(project_slot, (prefix_hidden, fresh_page))
    prefix_pages = jnp.where(cached[:, None, None], page_store[reuse[:, 1]], recomputed[reuse[:, 2]])
    prefix_rows = prefix_pages.reshape(PAGES * PAGE, KV_HEADS, 2 * HEAD_DIM)
    extension = ext_kv.reshape(KV_HEADS, EXT, 2 * HEAD_DIM)
    ext_positions = PREFIX + jnp.arange(EXT, dtype=jnp.int32)
    ext_keys = rotate(extension[:, :, :HEAD_DIM].transpose(1, 0, 2).astype(jnp.float32), ext_positions).astype(jnp.bfloat16)
    query_heads = queries.reshape(KV_HEADS, EXT, GQ, HEAD_DIM)
    block_rows = math.gcd(EXT, 512)
    block_count = EXT // block_rows
    key_positions = jnp.concatenate([jnp.full((PREFIX,), -1, jnp.int32), jnp.arange(EXT, dtype=jnp.int32)])
    outputs = []
    for head_index in range(KV_HEADS):
        all_keys = jnp.concatenate([prefix_rows[:, head_index, :HEAD_DIM], ext_keys[:, head_index, :]], axis=0).astype(jnp.float32)
        all_values = jnp.concatenate([prefix_rows[:, head_index, HEAD_DIM:], extension[head_index, :, HEAD_DIM:]], axis=0).astype(jnp.float32)
        rotated_queries = rotate(query_heads[head_index].astype(jnp.float32), ext_positions).astype(jnp.bfloat16)

        def attend(first_row):
            query_block = lax.dynamic_slice_in_dim(rotated_queries, first_row, block_rows, 0).astype(jnp.float32)
            scores = jnp.einsum('tgd,kd->gtk', query_block, all_keys) * (HEAD_DIM ** -0.5)
            query_positions = first_row + jnp.arange(block_rows, dtype=jnp.int32)
            visible = key_positions[None, :] <= query_positions[:, None]
            scores = jnp.where(visible[None], scores, MASK_VALUE)
            row_max = jnp.max(scores, axis=-1, keepdims=True)
            weights = jnp.exp(scores - row_max)
            weight_sum = jnp.sum(weights, axis=-1)
            rounded_weights = weights.astype(jnp.bfloat16).astype(jnp.float32)
            weighted = jnp.einsum('gtk,kd->gtd', rounded_weights, all_values)
            normed = weighted / weight_sum[..., None]
            return normed.transpose(1, 0, 2).reshape(block_rows, GQ * HEAD_DIM)

        block_starts = jnp.arange(block_count, dtype=jnp.int32) * block_rows
        outputs.append(lax.map(attend, block_starts).reshape(EXT, GQ * HEAD_DIM))
    return jnp.concatenate(outputs, axis=0).astype(jnp.bfloat16)
```

```python
import functools

import jax
import jax.numpy as jnp
from jax import lax
from jax.experimental import pallas as pl
from jax.experimental.pallas import tpu as pltpu
from jax.sharding import PartitionSpec as P

GQ = 5
HEAD_DIM = 128
PAIR = 2 * HEAD_DIM
HEADS = 4

ROPE_BASE = 1000000.0
MASK_VALUE = -1e30


def swap(value, axis, bit, count):
    return lax.ppermute(value, axis, [(i, i ^ bit) for i in range(count)])


def angle_tables(positions):
    half_dim = HEAD_DIM // 2
    frequency = ROPE_BASE ** (-jnp.arange(half_dim, dtype=jnp.float32) * 2.0 / HEAD_DIM)
    angles = positions.astype(jnp.float32)[..., None] * frequency
    cosine = jnp.cos(angles)
    sine = jnp.sin(angles)
    return (
        jnp.concatenate([cosine, cosine], axis=-1),
        jnp.concatenate([-sine, sine], axis=-1),
    )


def project_kernel(blocks, meta, *refs):
    pages, weights = refs[:4], refs[4:-6]
    bias, cosine, sine, out_first, out_second, total = refs[-6:]
    rows = cosine.shape[1]
    span = pages[0].shape[2] // blocks
    single = len(weights) == 1

    for block in range(blocks):
        chip = block if single else meta[2 + block]
        start = pl.multiple_of(chip * span, HEAD_DIM)
        left = jnp.concatenate([page[0, :, pl.ds(start, span)] for page in pages], axis=0)
        right = weights[0][pl.ds(block * span, span)] if single else weights[block][...]
        product = jnp.dot(left, right, preferred_element_type=jnp.float32)
        total[...] = product + (bias[...] if block == 0 else total[...])
    for out, place in ((out_first, 0), (out_second, 1)):
        base = meta[place] * 2
        for rel in range(2):
            page = total[pl.ds(pl.multiple_of((base + rel) * rows, rows), rows)]
            keys = page[:, :HEAD_DIM]
            turned = keys * cosine[base + rel] + pltpu.roll(keys, HEAD_DIM // 2, 1) * sine[
                base + rel
            ]
            out[rel, :, :HEAD_DIM] = turned.astype(jnp.bfloat16)
            out[rel, :, HEAD_DIM:] = page[:, HEAD_DIM:].astype(jnp.bfloat16)


def project(meta, pages, weights, bias, cosine, sine):
    rows, depth = pages[0].shape[1:]
    width = weights[0].shape[1]
    in_smem = pl.BlockSpec(memory_space=pltpu.SMEM)
    in_vmem = pl.BlockSpec(memory_space=pltpu.VMEM)
    return pl.pallas_call(
        functools.partial(project_kernel, 8),
        in_specs=[in_smem] + [in_vmem] * (4 + len(weights) + 3),
        out_specs=[in_vmem] * 2,
        out_shape=[jax.ShapeDtypeStruct((2, rows, width), jnp.bfloat16)] * 2,
        scratch_shapes=[pltpu.VMEM((4 * rows, width), jnp.float32)],
        compiler_params=pltpu.CompilerParams(vmem_limit_bytes=24 << 20),
        cost_estimate=pl.CostEstimate(
            flops=2 * 4 * rows * depth * width,
            bytes_accessed=2 * (4 * rows + width) * depth,
            transcendentals=0,
        ),
        name="project",
    )(meta, *pages, *weights, bias, cosine, sine)


def fold(query_ref, rows, top_ref, sum_ref, mask=None, first=False):
    key_rows, value_rows = rows[:, :HEAD_DIM], rows[:, HEAD_DIM:]
    copies = rows.shape[0] // HEAD_DIM
    extended = jnp.concatenate([value_rows, jnp.ones_like(value_rows)], axis=1)

    def scores_of(group):
        scores = lax.dot_general(
            query_ref[group],
            key_rows,
            (((1,), (1,)), ((), ())),
            preferred_element_type=jnp.float32,
        )
        return scores if mask is None else jnp.where(mask, scores, MASK_VALUE)

    ahead = scores_of(0)
    for group in range(GQ):
        scores = ahead
        if group + 1 < GQ:
            ahead = scores_of(group + 1)
        row_top = jnp.broadcast_to(
            jnp.max(scores, axis=1, keepdims=True), (scores.shape[0], HEAD_DIM)
        )
        if not first:
            old_top = top_ref[group]
            row_top = jnp.maximum(old_top, row_top)
        weights = jnp.exp(scores - jnp.concatenate([row_top] * copies, axis=1))
        product = jnp.dot(
            weights.astype(jnp.bfloat16), extended, preferred_element_type=jnp.float32
        )
        if not first:
            shrink = jnp.exp(old_top - row_top)
            product += sum_ref[group] * jnp.concatenate([shrink, shrink], axis=1)
        sum_ref[group] = product
        top_ref[group] = row_top


def fold_pages(query_ref, buffer, wait_page, count, top_ref, sum_ref):
    def part(start, size):
        for offset in range(size):
            wait_page(start + offset)
        rows = buffer[pl.ds(start, size)].reshape(size * buffer.shape[1], PAIR)
        fold(query_ref, rows, top_ref, sum_ref)

    full = count // 4

    def body(index, carry):
        part(index * 4, 4)
        return carry

    lax.fori_loop(0, full, body, 0)

    @pl.when((count & 2) != 0)
    def _():
        part(full * 4, 2)

    @pl.when((count & 1) != 0)
    def _():
        part(count - 1, 1)


def start_pages(reuse, flag, place, pieces, buffer, semaphores):
    page_count = reuse.shape[0]

    def body(page, count):
        chosen = reuse[page, 0] == flag

        @pl.when(chosen)
        def _():
            piece, index = place(reuse[page, 2 - flag])
            for number, source in enumerate(pieces):

                @pl.when(piece == number)
                def _():
                    pltpu.make_async_copy(
                        source.at[index], buffer.at[count], semaphores.at[count]
                    ).start()

        return count + chosen.astype(jnp.int32)

    return lax.fori_loop(0, page_count, body, jnp.int32(0))


def early_kernel(place, extension_at, count, slots, reuse, meta, query, cosine, sine, *refs):
    pieces = refs[:count]
    turned, top_ref, sum_ref, buffer, blocks, semaphores, block_semaphores = refs[count:]
    group_size, pages_each = blocks.shape[0], blocks.shape[1]
    slice_index = meta[1]

    def block_copy(relative):
        piece, index = extension_at(relative)
        return pltpu.make_async_copy(
            pieces[piece].at[pl.ds(index, pages_each)],
            blocks.at[relative],
            block_semaphores.at[relative],
        )

    for relative in range(group_size):
        block_copy(relative).start()
    found = start_pages(
        reuse, 1, functools.partial(place, slots, meta), pieces, buffer, semaphores
    )
    scale = HEAD_DIM**-0.5
    cos_rows, sin_rows = cosine[...], sine[...]
    for group in range(GQ):
        values = query[:, group * HEAD_DIM : (group + 1) * HEAD_DIM].astype(jnp.float32)
        rotated = values * cos_rows + pltpu.roll(values, HEAD_DIM // 2, 1) * sin_rows
        turned[group] = (rotated * scale).astype(jnp.bfloat16)

    row_count = query.shape[0]
    rows = lax.broadcasted_iota(jnp.int32, (row_count, row_count), 0)
    columns = lax.broadcasted_iota(jnp.int32, (row_count, row_count), 1)

    def attend(index, **options):
        fold(turned, blocks[index].reshape(row_count, PAIR), top_ref, sum_ref, **options)

    for relative in range(group_size):
        block_copy(relative).wait()
    attend(0, mask=columns <= rows, first=True)

    def earlier(index, carry):
        attend(index ^ slice_index)
        return carry

    lax.fori_loop(0, slice_index, earlier, 0)

    def wait_page(index):
        pltpu.make_async_copy(pieces[0].at[0], buffer.at[index], semaphores.at[index]).wait()

    fold_pages(turned, buffer, wait_page, found, top_ref, sum_ref)


def attend_early(
    place, extension_at, group_size, slots, reuse, meta, queries, row_cos, row_sin, pieces
):
    page_count, row_count, page_rows = reuse.shape[0], queries.shape[0], pieces[0].shape[1]
    in_smem = pl.BlockSpec(memory_space=pltpu.SMEM)
    in_vmem = pl.BlockSpec(memory_space=pltpu.VMEM)
    anywhere = pl.BlockSpec(memory_space=pl.ANY)
    shape = (GQ, row_count, HEAD_DIM)
    work = GQ * row_count * page_count * page_rows
    return pl.pallas_call(
        functools.partial(early_kernel, place, extension_at, len(pieces), slots),
        in_specs=[in_smem] * 2 + [in_vmem] * 3 + [anywhere] * len(pieces),
        out_specs=[in_vmem] * 3,
        out_shape=[
            jax.ShapeDtypeStruct(shape, jnp.bfloat16),
            jax.ShapeDtypeStruct(shape, jnp.float32),
            jax.ShapeDtypeStruct((GQ, row_count, PAIR), jnp.float32),
        ],
        scratch_shapes=[
            pltpu.VMEM((page_count, page_rows, PAIR), jnp.bfloat16),
            pltpu.VMEM((group_size, row_count // page_rows, page_rows, PAIR), jnp.bfloat16),
            pltpu.SemaphoreType.DMA((page_count,)),
            pltpu.SemaphoreType.DMA((group_size,)),
        ],
        compiler_params=pltpu.CompilerParams(vmem_limit_bytes=24 << 20),
        cost_estimate=pl.CostEstimate(
            flops=4 * work * HEAD_DIM,
            bytes_accessed=page_rows * page_count * PAIR * 2,
            transcendentals=work,
        ),
        name="early",
    )(reuse, meta, queries, row_cos, row_sin, *pieces)


def place_spread(group_size, slots, meta, slot):
    device = slot // slots
    return meta[1] ^ (device % group_size), device // group_size * slots + slot % slots


def place_apart(slots, meta, slot):
    device = slot // slots
    source, relative = device // 4, meta[1] ^ (device % 4)
    shift = (meta[0] - source) & 3
    return (relative & 1) * 2 + (relative >> 1), (shift ^ (shift >> 1)) * slots + slot % slots


def fresh_place(group_size, meta, device):
    source, spot = device // group_size, device % group_size
    holder = (spot - (spot & 1)) + (source & 1)
    index = ((source >> 1) ^ meta[2]) * 2 + ((spot ^ meta[0]) & 1)
    return meta[1] ^ holder, index


def late_kernel(group_size, reuse, meta, turned, top_in, sum_in, *refs):
    pieces = refs[:group_size]
    out, top_ref, sum_ref, buffer, semaphores = refs[group_size:]
    place = functools.partial(fresh_place, group_size, meta)
    count = start_pages(reuse, 0, place, pieces, buffer, semaphores)
    top_ref[...] = jnp.full_like(top_ref, MASK_VALUE)
    sum_ref[...] = jnp.zeros_like(sum_ref)

    def wait_page(index):
        pltpu.make_async_copy(pieces[0].at[0], buffer.at[index], semaphores.at[index]).wait()

    fold_pages(turned, buffer, wait_page, count, top_ref, sum_ref)
    for group in range(GQ):
        first_top, last_top = top_in[group], top_ref[group]
        row_top = jnp.maximum(first_top, last_top)
        first_share, last_share = jnp.exp(first_top - row_top), jnp.exp(last_top - row_top)
        total = sum_in[group] * jnp.concatenate([first_share, first_share], axis=1)
        total += sum_ref[group] * jnp.concatenate([last_share, last_share], axis=1)
        out[:, group * HEAD_DIM : (group + 1) * HEAD_DIM] = (
            total[:, :HEAD_DIM] / total[:, HEAD_DIM:]
        ).astype(out.dtype)


def attend_late(reuse, meta, turned, top, total, pieces):
    page_count, row_count, page_rows = reuse.shape[0], turned.shape[1], pieces[0].shape[1]
    group_size = len(pieces)
    most = min(page_count, group_size * pieces[0].shape[0])
    in_smem = pl.BlockSpec(memory_space=pltpu.SMEM)
    in_vmem = pl.BlockSpec(memory_space=pltpu.VMEM)
    anywhere = pl.BlockSpec(memory_space=pl.ANY)
    work = GQ * row_count * page_rows * page_count // 2
    return pl.pallas_call(
        functools.partial(late_kernel, group_size),
        in_specs=[in_smem] * 2 + [in_vmem] * 3 + [anywhere] * group_size,
        out_specs=in_vmem,
        out_shape=jax.ShapeDtypeStruct((row_count, GQ * HEAD_DIM), jnp.bfloat16),
        scratch_shapes=[
            pltpu.VMEM(top.shape, top.dtype),
            pltpu.VMEM(total.shape, total.dtype),
            pltpu.VMEM((most, page_rows, PAIR), jnp.bfloat16),
            pltpu.SemaphoreType.DMA((most,)),
        ],
        compiler_params=pltpu.CompilerParams(vmem_limit_bytes=24 << 20),
        cost_estimate=pl.CostEstimate(
            flops=4 * work * HEAD_DIM,
            bytes_accessed=page_rows * page_count * PAIR,
            transcendentals=work,
        ),
        name="late",
    )(reuse, meta, turned, top, total, *pieces)


def on_device(parts, queries, ext_kv, page_store, prefix_hidden, kv_weight, kv_bias, reuse):
    devices = lax.axis_size("kv")
    own_index = lax.axis_index("kv")
    part_index = lax.axis_index("grp")
    row_count = queries.shape[0]
    group_size = devices // HEADS
    group_bits = group_size.bit_length() - 1
    head = own_index >> group_bits
    slice_index = own_index & (group_size - 1)
    core = own_index & 1
    side = part_index & 1
    page_count = reuse.shape[0]
    slots, page_rows = page_store.shape[0], page_store.shape[1]

    def exchange(value, bit):
        return swap(value, "kv", bit, devices)

    def between_planes(value):
        groups = [list(range(spot, devices, group_size)) for spot in range(group_size)]
        return lax.all_to_all(value, "kv", 0, 0, axis_index_groups=groups, tiled=True)

    hidden_across = swap(prefix_hidden, "grp", 1, parts)

    target = 2 * side + core
    spare = 2 * side + (1 - core)
    mine = lax.dynamic_slice_in_dim(kv_weight, target * PAIR, PAIR, 1)
    other = exchange(lax.dynamic_slice_in_dim(kv_weight, spare * PAIR, PAIR, 1), 1)
    chip_rows = jnp.where(
        core == 0,
        jnp.concatenate([mine, other], axis=0),
        jnp.concatenate([other, mine], axis=0),
    )

    def as_pages(*blocks):
        return jnp.concatenate(blocks, axis=0).reshape(-1, page_rows, PAIR)

    def stored_for(store, plane):
        part = lax.dynamic_slice_in_dim(store, plane * PAIR, PAIR, 2)
        return part.reshape(slots * page_rows, PAIR)

    order = []
    if group_size == 4:
        def to_plane(value, shift):
            step = shift * group_size
            return lax.ppermute(value, "kv", [(i, (i + step) % devices) for i in range(devices)])

        own_part = stored_for(page_store, head)
        others = [
            to_plane(stored_for(page_store, (head + shift) & (HEADS - 1)), shift)
            for shift in (1, 3, 2)
        ]
        near = to_plane(chip_rows, 1)
        again, others = lax.optimization_barrier((chip_rows, others))
        back = to_plane(again, 3)
        beside_own = exchange(chip_rows, 2)
        far = to_plane(near, 1)
        near_sent, _ = lax.optimization_barrier((near, beside_own))
        beside_near = exchange(near_sent, 2)
        back_sent, _ = lax.optimization_barrier((back, beside_near))
        beside_back = exchange(back_sent, 2)
        far_sent, hidden_mine, hidden_passed, reuse_sent, _ = lax.optimization_barrier(
            (far, prefix_hidden, hidden_across, reuse, beside_back)
        )
        hidden_core = exchange(hidden_mine, 1)
        beside_far = exchange(far_sent, 2)
        weights = [chip_rows, beside_own, near, beside_near, back, beside_back, far, beside_far]
        for shift in (0, 1, 3, 2):
            chip = (((head - shift) & (HEADS - 1)) << 1) | (slice_index >> 1)
            order += [chip, chip ^ 1]
    else:
        hidden_core, hidden_passed, reuse_sent = exchange(prefix_hidden, 1), hidden_across, reuse
        weights = [
            lax.all_gather(
                chip_rows,
                "kv",
                axis=0,
                tiled=True,
                axis_index_groups=[list(range(first, devices, 2)) for first in range(2)],
            )
        ]
    hidden_diagonal = exchange(hidden_passed, 1)
    reuse_across = swap(reuse_sent, "grp", 1, parts)
    offset = page_count * page_rows
    (ext_kv, first_row), _ = lax.optimization_barrier(
        ((ext_kv, slice_index * row_count), weights[min(2, len(weights) - 1)])
    )
    query_pos = offset + first_row + jnp.arange(row_count, dtype=jnp.int32)
    row_cos, row_sin = angle_tables(query_pos)
    raw_keys = ext_kv[:, :HEAD_DIM].astype(jnp.float32)
    own_keys = raw_keys * row_cos + jnp.roll(raw_keys, HEAD_DIM // 2, axis=1) * row_sin
    own_block = jnp.concatenate([own_keys.astype(jnp.bfloat16), ext_kv[:, HEAD_DIM:]], axis=1)

    if group_size == 4:
        gathered, beside_far = lax.optimization_barrier(
            (as_pages(own_part, *others, own_block), weights[-1])
        )
        gathered_beside = exchange(gathered, 2)

    def page_numbers(table):
        match = (table[:, 0] == 0)[:, None] & (
            table[:, 2][:, None] == jnp.stack([own_index, own_index ^ 1])[None, :]
        )
        return jnp.sum(
            jnp.where(match, jnp.arange(page_count, dtype=jnp.int32)[:, None], 0), axis=0
        )

    numbers = jnp.concatenate([page_numbers(reuse), page_numbers(reuse_across)])
    page_cos, page_sin = angle_tables(
        numbers[:, None] * page_rows + jnp.arange(page_rows, dtype=jnp.int32)[None, :]
    )

    bias = lax.dynamic_slice_in_dim(kv_bias, target * PAIR, PAIR, 0).astype(jnp.float32)[None, :]
    first_side = (head >> 1) ^ side
    choice = jnp.stack([first_side, first_side ^ 1] + order).astype(jnp.int32)
    messages = project(
        choice,
        (prefix_hidden, hidden_core, hidden_across, hidden_diagonal),
        weights,
        bias,
        page_cos,
        page_sin,
    )
    received = []
    for turn, message in enumerate(messages):
        routes = []
        for part in range(parts):
            for device in range(devices):
                plane, spot = device // group_size, device % group_size
                to_part = (part & ~1) | ((plane >> 1) ^ turn)
                to_spot = (spot & ~1) | (plane & 1)
                to_head = 2 * (part & 1) + (spot & 1)
                routes.append(
                    (part * devices + device, to_part * devices + to_head * group_size + to_spot)
                )
        received.append(lax.ppermute(message, ("grp", "kv"), routes))
    meta = jnp.stack([head, slice_index, side]).astype(jnp.int32)
    bits = []
    while 1 << len(bits) < group_size:
        bits.insert(0, 1 << len(bits))

    def spread(own, first):
        pieces = {0: own, bits[0]: first}
        for bit in bits[1:]:
            pieces.update({known ^ bit: exchange(value, bit) for known, value in pieces.items()})
        return [pieces[relative] for relative in range(group_size)]

    if group_size == 4:
        pieces, _ = lax.optimization_barrier(([gathered, gathered_beside], received))
        pieces += [exchange(piece, 1) for piece in pieces]
        place = place_apart
        extension_at = lambda relative: ((relative & 1) * 2 + (relative >> 1), HEADS * slots)
    else:
        per_head = page_store.reshape(slots, page_rows, HEADS, PAIR).transpose(2, 0, 1, 3)
        arrived = between_planes(per_head.reshape(HEADS * slots, page_rows, PAIR))
        gathered = as_pages(arrived.reshape(-1, PAIR), own_block)
        pieces = spread(gathered, exchange(gathered, bits[0]))
        place = functools.partial(place_spread, group_size)
        extension_at = lambda relative: (relative, HEADS * slots)
    turned, top, total = attend_early(
        place, extension_at, group_size, slots, reuse, meta, queries, row_cos, row_sin, pieces
    )
    late_own = jnp.concatenate(received, axis=0)
    late_first = exchange(late_own, bits[0])
    late_first, turned = lax.optimization_barrier((late_first, turned))
    late_pieces = spread(late_own, late_first)
    return attend_late(reuse, meta, turned, top, total, late_pieces)


def solution(mesh):
    placed = (
        P(("grp", "kv"), None),
        P(("grp", "kv"), None),
        P(("grp", "kv"), None, None),
        P(("grp", "kv"), None, None),
        P("kv", None),
        P(),
        P("grp", None),
    )
    return jax.shard_map(
        functools.partial(on_device, mesh.shape["grp"]),
        mesh=mesh,
        in_specs=placed,
        out_specs=P(("grp", "kv"), None),
        check_vma=False,
    )
```

```python
import functools

import jax
import jax.numpy as jnp
from jax import lax
from jax.experimental import pallas as pl
from jax.experimental.pallas import tpu as pltpu
from jax.sharding import PartitionSpec as P

GQ = 5
HEAD_DIM = 128
PAIR = 2 * HEAD_DIM
HEADS = 4

ROPE_BASE = 1000000.0
MASK_VALUE = -1e30


def swap(value, axis, bit, count):
    return lax.ppermute(value, axis, [(i, i ^ bit) for i in range(count)])


def angle_tables(positions):
    half_dim = HEAD_DIM // 2
    frequency = ROPE_BASE ** (-jnp.arange(half_dim, dtype=jnp.float32) * 2.0 / HEAD_DIM)
    angles = positions.astype(jnp.float32)[..., None] * frequency
    cosine = jnp.cos(angles)
    sine = jnp.sin(angles)
    return (
        jnp.concatenate([cosine, cosine], axis=-1),
        jnp.concatenate([-sine, sine], axis=-1),
    )


def project_kernel(blocks, meta, *refs):
    pages, weights = refs[:4], refs[4:-10]
    store, store_across, store_core, bias, cosine, sine = refs[-10:-4]
    out_first, out_second, total, stored = refs[-4:]
    rows = cosine.shape[1]
    span = pages[0].shape[2] // blocks
    single = len(weights) == 1

    for block in range(blocks):
        chip = block if single else meta[12 + block]
        start = pl.multiple_of(chip * span, HEAD_DIM)
        left = jnp.concatenate([page[0, :, pl.ds(start, span)] for page in pages], axis=0)
        right = weights[0][pl.ds(block * span, span)] if single else weights[block][...]
        product = jnp.dot(left, right, preferred_element_type=jnp.float32)
        total[...] = product + (bias[...] if block == 0 else total[...])
    core, target = meta[2], meta[3]
    for slot in range(2):
        stored[0, slot] = store[slot, :, pl.ds(pl.multiple_of(target * PAIR, PAIR), PAIR)]
        stored[1, slot] = store_core[slot]
        stored[2, slot] = store_across[slot, :, pl.ds(pl.multiple_of(core * PAIR, PAIR), PAIR)]
        stored[3, slot] = store_core[2 + slot]
    for out, place in ((out_first, 0), (out_second, 1)):
        base = meta[place] * 2
        for rel in range(2):
            number = base + rel
            page = total[pl.ds(pl.multiple_of(number * rows, rows), rows)]
            keys = page[:, :HEAD_DIM]
            turned = keys * cosine[number] + pltpu.roll(keys, HEAD_DIM // 2, 1) * sine[number]
            fresh = meta[4 + number] > 0
            swapped = fresh & (meta[8 + number] == 0)
            out[2 * rel] = stored[number, swapped.astype(jnp.int32)]

            @pl.when(fresh)
            def _():
                out[2 * rel + 1, :, :HEAD_DIM] = turned.astype(jnp.bfloat16)
                out[2 * rel + 1, :, HEAD_DIM:] = page[:, HEAD_DIM:].astype(jnp.bfloat16)

            @pl.when(jnp.logical_not(fresh))
            def _():
                out[2 * rel + 1] = stored[number, 1]


def project(meta, pages, weights, stores, bias, cosine, sine):
    rows, depth = pages[0].shape[1:]
    width = weights[0].shape[1]
    in_smem = pl.BlockSpec(memory_space=pltpu.SMEM)
    in_vmem = pl.BlockSpec(memory_space=pltpu.VMEM)
    return pl.pallas_call(
        functools.partial(project_kernel, 8),
        in_specs=[in_smem] + [in_vmem] * (4 + len(weights) + 6),
        out_specs=[in_vmem] * 2,
        out_shape=[jax.ShapeDtypeStruct((4, rows, width), jnp.bfloat16)] * 2,
        scratch_shapes=[
            pltpu.VMEM((4 * rows, width), jnp.float32),
            pltpu.VMEM((4, 2, rows, width), jnp.bfloat16),
        ],
        compiler_params=pltpu.CompilerParams(vmem_limit_bytes=24 << 20),
        cost_estimate=pl.CostEstimate(
            flops=2 * 4 * rows * depth * width,
            bytes_accessed=2 * (4 * rows + width) * depth,
            transcendentals=0,
        ),
        name="project",
    )(meta, *pages, *weights, *stores, bias, cosine, sine)


def fold(query_ref, rows, top_ref, sum_ref, mask=None, first=False):
    key_rows, value_rows = rows[:, :HEAD_DIM], rows[:, HEAD_DIM:]
    copies = rows.shape[0] // HEAD_DIM
    extended = jnp.concatenate([value_rows, jnp.ones_like(value_rows)], axis=1)

    def scores_of(group):
        scores = lax.dot_general(
            query_ref[group],
            key_rows,
            (((1,), (1,)), ((), ())),
            preferred_element_type=jnp.float32,
        )
        return scores if mask is None else jnp.where(mask, scores, MASK_VALUE)

    ahead = scores_of(0)
    for group in range(GQ):
        scores = ahead
        if group + 1 < GQ:
            ahead = scores_of(group + 1)
        row_top = jnp.broadcast_to(
            jnp.max(scores, axis=1, keepdims=True), (scores.shape[0], HEAD_DIM)
        )
        if not first:
            old_top = top_ref[group]
            row_top = jnp.maximum(old_top, row_top)
        weights = jnp.exp(scores - jnp.concatenate([row_top] * copies, axis=1))
        product = jnp.dot(
            weights.astype(jnp.bfloat16), extended, preferred_element_type=jnp.float32
        )
        if not first:
            shrink = jnp.exp(old_top - row_top)
            product += sum_ref[group] * jnp.concatenate([shrink, shrink], axis=1)
        sum_ref[group] = product
        top_ref[group] = row_top


def fold_pages(query_ref, buffer, wait_page, count, top_ref, sum_ref):
    def part(start, size):
        for offset in range(size):
            wait_page(start + offset)
        rows = buffer[pl.ds(start, size)].reshape(size * buffer.shape[1], PAIR)
        fold(query_ref, rows, top_ref, sum_ref)

    full = count // 4

    def body(index, carry):
        part(index * 4, 4)
        return carry

    lax.fori_loop(0, full, body, 0)

    @pl.when((count & 2) != 0)
    def _():
        part(full * 4, 2)

    @pl.when((count & 1) != 0)
    def _():
        part(count - 1, 1)


def extension_kernel(group_size, meta, query, cosine, sine, *refs):
    pieces, (turned, top_ref, sum_ref) = refs[:group_size], refs[group_size:]
    slice_index = meta[1]
    scale = HEAD_DIM**-0.5
    cos_rows, sin_rows = cosine[...], sine[...]
    for group in range(GQ):
        values = query[:, group * HEAD_DIM : (group + 1) * HEAD_DIM].astype(jnp.float32)
        rotated = values * cos_rows + pltpu.roll(values, HEAD_DIM // 2, 1) * sin_rows
        turned[group] = (rotated * scale).astype(jnp.bfloat16)
    row_count = query.shape[0]
    rows = lax.broadcasted_iota(jnp.int32, (row_count, row_count), 0)
    columns = lax.broadcasted_iota(jnp.int32, (row_count, row_count), 1)

    fold(turned, pieces[0][...], top_ref, sum_ref, mask=columns <= rows, first=True)
    for relative in range(1, group_size):

        @pl.when((slice_index ^ relative) < slice_index)
        def _():
            fold(turned, pieces[relative][...], top_ref, sum_ref)


def attend_extension(meta, queries, row_cos, row_sin, pieces):
    row_count = queries.shape[0]
    in_smem = pl.BlockSpec(memory_space=pltpu.SMEM)
    in_vmem = pl.BlockSpec(memory_space=pltpu.VMEM)
    shape = (GQ, row_count, HEAD_DIM)
    work = GQ * row_count * row_count * len(pieces)
    return pl.pallas_call(
        functools.partial(extension_kernel, len(pieces)),
        in_specs=[in_smem] + [in_vmem] * (3 + len(pieces)),
        out_specs=[in_vmem] * 3,
        out_shape=[
            jax.ShapeDtypeStruct(shape, jnp.bfloat16),
            jax.ShapeDtypeStruct(shape, jnp.float32),
            jax.ShapeDtypeStruct((GQ, row_count, PAIR), jnp.float32),
        ],
        compiler_params=pltpu.CompilerParams(vmem_limit_bytes=24 << 20),
        cost_estimate=pl.CostEstimate(
            flops=4 * work * HEAD_DIM,
            bytes_accessed=row_count * PAIR * 2 * len(pieces),
            transcendentals=work,
        ),
        name="extension",
    )(meta, queries, row_cos, row_sin, *pieces)


def pages_kernel(
    group_size, beside, last, reuse, meta, turned, top_in, sum_in, *refs
):
    count_pieces = group_size // 2
    pieces, outs = refs[:count_pieces], refs[count_pieces : count_pieces + (1 if last else 2)]
    top_ref, sum_ref, buffer, in_use, semaphores = refs[-5:]
    page_count, devices = reuse.shape[0], in_use.shape[0]
    head, slice_index, side = meta[0], meta[1], meta[2]

    def clear(device, carry):
        in_use[device] = 0
        return carry

    lax.fori_loop(0, devices, clear, 0)

    def note(page, carry):
        @pl.when(reuse[page, 0] == 0)
        def _():
            in_use[reuse[page, 2]] = 1

        return carry

    lax.fori_loop(0, page_count, note, 0)

    def start(page, count):
        cached = reuse[page, 0] == 1
        slot = reuse[page, 1]
        device = jnp.where(cached, slot >> 1, reuse[page, 2])
        source, spot = device // group_size, device % group_size
        holder = (spot - (spot & 1)) + (source & 1)
        relative = slice_index ^ holder
        half = jnp.where(
            cached, jnp.where((slot & 1) == 0, 0, 1 - in_use[device]), 1
        )
        index = (((source >> 1) ^ side) * 2 + ((spot ^ head) & 1)) * 2 + half
        chosen = (relative & (group_size // 2)) == (group_size // 2 if beside else 0)

        @pl.when(chosen)
        def _():
            for number, piece in enumerate(pieces):

                @pl.when((relative & (group_size // 2 - 1)) == number)
                def _():
                    pltpu.make_async_copy(
                        piece.at[index], buffer.at[count], semaphores.at[count]
                    ).start()

        return count + chosen.astype(jnp.int32)

    count = lax.fori_loop(0, page_count, start, jnp.int32(0))
    top_ref[...] = jnp.full_like(top_ref, MASK_VALUE)
    sum_ref[...] = jnp.zeros_like(sum_ref)

    def wait_page(index):
        pltpu.make_async_copy(pieces[0].at[0], buffer.at[index], semaphores.at[index]).wait()

    fold_pages(turned, buffer, wait_page, count, top_ref, sum_ref)
    for group in range(GQ):
        first_top, last_top = top_in[group], top_ref[group]
        row_top = jnp.maximum(first_top, last_top)
        first_share, last_share = jnp.exp(first_top - row_top), jnp.exp(last_top - row_top)
        total = sum_in[group] * jnp.concatenate([first_share, first_share], axis=1)
        total += sum_ref[group] * jnp.concatenate([last_share, last_share], axis=1)
        if last:
            outs[0][:, group * HEAD_DIM : (group + 1) * HEAD_DIM] = (
                total[:, :HEAD_DIM] / total[:, HEAD_DIM:]
            ).astype(outs[0].dtype)
        else:
            outs[0][group] = row_top
            outs[1][group] = total


def attend_pages(group_size, devices, last, reuse, meta, turned, top, total, pieces):
    page_count, row_count, page_rows = reuse.shape[0], turned.shape[1], pieces[0].shape[1]
    most = min(page_count, len(pieces) * pieces[0].shape[0])
    in_smem = pl.BlockSpec(memory_space=pltpu.SMEM)
    in_vmem = pl.BlockSpec(memory_space=pltpu.VMEM)
    anywhere = pl.BlockSpec(memory_space=pl.ANY)
    work = GQ * row_count * page_rows * page_count // 2
    state = [
        jax.ShapeDtypeStruct(top.shape, top.dtype),
        jax.ShapeDtypeStruct(total.shape, total.dtype),
    ]
    final = [jax.ShapeDtypeStruct((row_count, GQ * HEAD_DIM), jnp.bfloat16)]
    return pl.pallas_call(
        functools.partial(pages_kernel, group_size, last, last),
        in_specs=[in_smem] * 2 + [in_vmem] * 3 + [anywhere] * len(pieces),
        out_specs=[in_vmem] if last else [in_vmem] * 2,
        out_shape=final if last else state,
        scratch_shapes=[
            pltpu.VMEM(top.shape, top.dtype),
            pltpu.VMEM(total.shape, total.dtype),
            pltpu.VMEM((most, page_rows, PAIR), jnp.bfloat16),
            pltpu.SMEM((devices,), jnp.int32),
            pltpu.SemaphoreType.DMA((most,)),
        ],
        compiler_params=pltpu.CompilerParams(vmem_limit_bytes=24 << 20),
        cost_estimate=pl.CostEstimate(
            flops=4 * work * HEAD_DIM,
            bytes_accessed=page_rows * page_count * PAIR,
            transcendentals=work,
        ),
        name="beside" if last else "column",
    )(reuse, meta, turned, top, total, *pieces)


def on_device(parts, queries, ext_kv, page_store, prefix_hidden, kv_weight, kv_bias, reuse):
    devices = lax.axis_size("kv")
    own_index = lax.axis_index("kv")
    part_index = lax.axis_index("grp")
    row_count = queries.shape[0]
    group_size = devices // HEADS
    group_bits = group_size.bit_length() - 1
    head = own_index >> group_bits
    slice_index = own_index & (group_size - 1)
    core = own_index & 1
    side = part_index & 1
    page_count = reuse.shape[0]
    slots, page_rows = page_store.shape[0], page_store.shape[1]

    def exchange(value, bit):
        return swap(value, "kv", bit, devices)

    hidden_across = swap(prefix_hidden, "grp", 1, parts)

    target = 2 * side + core
    spare = 2 * side + (1 - core)
    mine = lax.dynamic_slice_in_dim(kv_weight, target * PAIR, PAIR, 1)
    other = exchange(lax.dynamic_slice_in_dim(kv_weight, spare * PAIR, PAIR, 1), 1)
    chip_rows = jnp.where(
        core == 0,
        jnp.concatenate([mine, other], axis=0),
        jnp.concatenate([other, mine], axis=0),
    )

    order = []
    if group_size == 4:
        def to_plane(value, shift):
            step = shift * group_size
            return lax.ppermute(value, "kv", [(i, (i + step) % devices) for i in range(devices)])

        near, back = to_plane(chip_rows, 1), to_plane(chip_rows, 3)
        beside_own = exchange(chip_rows, 2)
        far = to_plane(near, 1)
        near_sent, _ = lax.optimization_barrier((near, beside_own))
        beside_near = exchange(near_sent, 2)
        back_sent, _ = lax.optimization_barrier((back, beside_near))
        beside_back = exchange(back_sent, 2)
        far_sent, hidden_mine, hidden_passed, reuse_sent, store_sent, _ = (
            lax.optimization_barrier(
                (far, prefix_hidden, hidden_across, reuse, page_store, beside_back)
            )
        )
        hidden_core = exchange(hidden_mine, 1)
        beside_far = exchange(far_sent, 2)
        weights = [chip_rows, beside_own, near, beside_near, back, beside_back, far, beside_far]
        for shift in (0, 1, 3, 2):
            chip = (((head - shift) & (HEADS - 1)) << 1) | (slice_index >> 1)
            order += [chip, chip ^ 1]
    else:
        hidden_core, hidden_passed = exchange(prefix_hidden, 1), hidden_across
        reuse_sent, store_sent = reuse, page_store
        weights = [
            lax.all_gather(
                chip_rows,
                "kv",
                axis=0,
                tiled=True,
                axis_index_groups=[list(range(first, devices, 2)) for first in range(2)],
            )
        ]
    hidden_diagonal = exchange(hidden_passed, 1)
    reuse_across = swap(reuse_sent, "grp", 1, parts)
    offset = page_count * page_rows
    (ext_kv, first_row), _ = lax.optimization_barrier(
        ((ext_kv, slice_index * row_count), weights[min(2, len(weights) - 1)])
    )
    query_pos = offset + first_row + jnp.arange(row_count, dtype=jnp.int32)
    row_cos, row_sin = angle_tables(query_pos)
    raw_keys = ext_kv[:, :HEAD_DIM].astype(jnp.float32)
    own_keys = raw_keys * row_cos + jnp.roll(raw_keys, HEAD_DIM // 2, axis=1) * row_sin
    own_block = jnp.concatenate([own_keys.astype(jnp.bfloat16), ext_kv[:, HEAD_DIM:]], axis=1)

    bits = []
    while 1 << len(bits) < group_size:
        bits.insert(0, 1 << len(bits))

    def spread(pieces, bits):
        pieces = dict(pieces)
        for bit in bits:
            pieces.update({known ^ bit: exchange(value, bit) for known, value in pieces.items()})
        return [pieces[relative] for relative in sorted(pieces)]

    meta = jnp.stack([head, slice_index, side]).astype(jnp.int32)
    turned, top, total = attend_extension(
        meta, queries, row_cos, row_sin, spread({0: own_block}, bits)
    )
    hidden_diagonal, turned = lax.optimization_barrier((hidden_diagonal, turned))

    other_part = lax.dynamic_slice_in_dim(store_sent, (1 - side) * 2 * PAIR, 2 * PAIR, 2)
    store_across = swap(other_part, "grp", 1, parts)
    store_core = exchange(
        jnp.concatenate(
            [
                lax.dynamic_slice_in_dim(page_store, spare * PAIR, PAIR, 2),
                lax.dynamic_slice_in_dim(store_across, (1 - core) * PAIR, PAIR, 2),
            ],
            axis=0,
        ),
        1,
    )

    def page_numbers(table):
        match = (table[:, 0] == 0)[:, None] & (
            table[:, 2][:, None] == jnp.stack([own_index, own_index ^ 1])[None, :]
        )
        return jnp.sum(
            jnp.where(match, jnp.arange(page_count, dtype=jnp.int32)[:, None], 0), axis=0
        )

    def in_use(table):
        pair = jnp.stack([own_index, own_index ^ 1])[None, :]
        cached = (table[:, 0] == 1)[:, None]
        fresh = jnp.any(jnp.logical_not(cached) & (table[:, 2][:, None] == pair), axis=0)
        first = jnp.any(cached & (table[:, 1][:, None] == 2 * pair), axis=0)
        return fresh.astype(jnp.int32), first.astype(jnp.int32)

    numbers = jnp.concatenate([page_numbers(reuse), page_numbers(reuse_across)])
    flags = [jnp.concatenate(pair) for pair in zip(in_use(reuse), in_use(reuse_across))]
    page_cos, page_sin = angle_tables(
        numbers[:, None] * page_rows + jnp.arange(page_rows, dtype=jnp.int32)[None, :]
    )

    bias = lax.dynamic_slice_in_dim(kv_bias, target * PAIR, PAIR, 0).astype(jnp.float32)[None, :]
    first_side = (head >> 1) ^ side
    choice = jnp.concatenate(
        [jnp.stack([first_side, first_side ^ 1, core, target]), *flags]
        + ([jnp.stack(order)] if order else [])
    ).astype(jnp.int32)
    messages = project(
        choice,
        (prefix_hidden, hidden_core, hidden_across, hidden_diagonal),
        weights,
        (page_store, store_across, store_core),
        bias,
        page_cos,
        page_sin,
    )
    received = []
    for turn, message in enumerate(messages):
        routes = []
        for part in range(parts):
            for device in range(devices):
                plane, spot = device // group_size, device % group_size
                to_part = (part & ~1) | ((plane >> 1) ^ turn)
                to_spot = (spot & ~1) | (plane & 1)
                to_head = 2 * (part & 1) + (spot & 1)
                routes.append(
                    (part * devices + device, to_part * devices + to_head * group_size + to_spot)
                )
        received.append(lax.ppermute(message, ("grp", "kv"), routes))
    arrived = jnp.concatenate(received, axis=0)
    crossed = exchange(arrived, bits[0])
    top, total = attend_pages(
        group_size, devices, False, reuse, meta, turned, top, total,
        spread({0: arrived}, bits[1:]),
    )
    crossed, top = lax.optimization_barrier((crossed, top))
    return attend_pages(
        group_size, devices, True, reuse, meta, turned, top, total,
        spread({0: crossed}, bits[1:]),
    )[0]


def solution(mesh):
    placed = (
        P(("grp", "kv"), None),
        P(("grp", "kv"), None),
        P(("grp", "kv"), None, None),
        P(("grp", "kv"), None, None),
        P("kv", None),
        P(),
        P("grp", None),
    )
    return jax.shard_map(
        functools.partial(on_device, mesh.shape["grp"]),
        mesh=mesh,
        in_specs=placed,
        out_specs=P(("grp", "kv"), None),
        check_vma=False,
    )
```

```python
import functools

import jax
import jax.numpy as jnp
from jax import lax
from jax.experimental import pallas as pl
from jax.experimental.pallas import tpu as pltpu
from jax.sharding import PartitionSpec as P

GQ = 5
HEAD_DIM = 128
PAIR = 2 * HEAD_DIM
HEADS = 4

ROPE_BASE = 1000000.0
MASK_VALUE = -1e30


def swap(value, axis, bit, count):
    return lax.ppermute(value, axis, [(i, i ^ bit) for i in range(count)])


def angle_tables(positions):
    half_dim = HEAD_DIM // 2
    frequency = ROPE_BASE ** (-jnp.arange(half_dim, dtype=jnp.float32) * 2.0 / HEAD_DIM)
    angles = positions.astype(jnp.float32)[..., None] * frequency
    cosine = jnp.cos(angles)
    sine = jnp.sin(angles)
    return (
        jnp.concatenate([cosine, cosine], axis=-1),
        jnp.concatenate([-sine, sine], axis=-1),
    )


def project_kernel(blocks, meta, *refs):
    pages, weights = refs[:4], refs[4:-6]
    bias, cosine, sine, out_first, out_second, total = refs[-6:]
    rows = cosine.shape[1]
    span = pages[0].shape[2] // blocks
    single = len(weights) == 1

    for block in range(blocks):
        chip = block if single else meta[2 + block]
        start = pl.multiple_of(chip * span, HEAD_DIM)
        left = jnp.concatenate([page[0, :, pl.ds(start, span)] for page in pages], axis=0)
        right = weights[0][pl.ds(block * span, span)] if single else weights[block][...]
        product = jnp.dot(left, right, preferred_element_type=jnp.float32)
        total[...] = product + (bias[...] if block == 0 else total[...])
    for out, place in ((out_first, 0), (out_second, 1)):
        base = meta[place] * 2
        for rel in range(2):
            page = total[pl.ds(pl.multiple_of((base + rel) * rows, rows), rows)]
            keys = page[:, :HEAD_DIM]
            turned = keys * cosine[base + rel] + pltpu.roll(keys, HEAD_DIM // 2, 1) * sine[
                base + rel
            ]
            out[rel, :, :HEAD_DIM] = turned.astype(jnp.bfloat16)
            out[rel, :, HEAD_DIM:] = page[:, HEAD_DIM:].astype(jnp.bfloat16)


def project(meta, pages, weights, bias, cosine, sine):
    rows, depth = pages[0].shape[1:]
    width = weights[0].shape[1]
    in_smem = pl.BlockSpec(memory_space=pltpu.SMEM)
    in_vmem = pl.BlockSpec(memory_space=pltpu.VMEM)
    return pl.pallas_call(
        functools.partial(project_kernel, 8),
        in_specs=[in_smem] + [in_vmem] * (4 + len(weights) + 3),
        out_specs=[in_vmem] * 2,
        out_shape=[jax.ShapeDtypeStruct((2, rows, width), jnp.bfloat16)] * 2,
        scratch_shapes=[pltpu.VMEM((4 * rows, width), jnp.float32)],
        compiler_params=pltpu.CompilerParams(vmem_limit_bytes=24 << 20),
        cost_estimate=pl.CostEstimate(
            flops=2 * 4 * rows * depth * width,
            bytes_accessed=2 * (4 * rows + width) * depth,
            transcendentals=0,
        ),
        name="project",
    )(meta, *pages, *weights, bias, cosine, sine)


def fold(query_ref, rows, top_ref, sum_ref, mask=None, first=False):
    key_rows, value_rows = rows[:, :HEAD_DIM], rows[:, HEAD_DIM:]
    copies = rows.shape[0] // HEAD_DIM
    extended = jnp.concatenate([value_rows, jnp.ones_like(value_rows)], axis=1)

    def scores_of(group):
        scores = lax.dot_general(
            query_ref[group],
            key_rows,
            (((1,), (1,)), ((), ())),
            preferred_element_type=jnp.float32,
        )
        return scores if mask is None else jnp.where(mask, scores, MASK_VALUE)

    ahead = scores_of(0)
    for group in range(GQ):
        scores = ahead
        if group + 1 < GQ:
            ahead = scores_of(group + 1)
        row_top = jnp.broadcast_to(
            jnp.max(scores, axis=1, keepdims=True), (scores.shape[0], HEAD_DIM)
        )
        if not first:
            old_top = top_ref[group]
            row_top = jnp.maximum(old_top, row_top)
        weights = jnp.exp(scores - jnp.concatenate([row_top] * copies, axis=1))
        product = jnp.dot(
            weights.astype(jnp.bfloat16), extended, preferred_element_type=jnp.float32
        )
        if not first:
            shrink = jnp.exp(old_top - row_top)
            product += sum_ref[group] * jnp.concatenate([shrink, shrink], axis=1)
        sum_ref[group] = product
        top_ref[group] = row_top


def fold_pages(query_ref, buffer, wait_page, count, top_ref, sum_ref):
    def part(start, size):
        for offset in range(size):
            wait_page(start + offset)
        rows = buffer[pl.ds(start, size)].reshape(size * buffer.shape[1], PAIR)
        fold(query_ref, rows, top_ref, sum_ref)

    full = count // 4

    def body(index, carry):
        part(index * 4, 4)
        return carry

    lax.fori_loop(0, full, body, 0)

    @pl.when((count & 2) != 0)
    def _():
        part(full * 4, 2)

    @pl.when((count & 1) != 0)
    def _():
        part(count - 1, 1)


def start_pages(reuse, flag, place, pieces, buffer, semaphores):
    page_count = reuse.shape[0]

    def body(page, count):
        chosen = reuse[page, 0] == flag

        @pl.when(chosen)
        def _():
            piece, index = place(reuse[page, 2 - flag])
            for number, source in enumerate(pieces):

                @pl.when(piece == number)
                def _():
                    pltpu.make_async_copy(
                        source.at[index], buffer.at[count], semaphores.at[count]
                    ).start()

        return count + chosen.astype(jnp.int32)

    return lax.fori_loop(0, page_count, body, jnp.int32(0))


def early_kernel(place, extension_at, count, slots, reuse, meta, query, cosine, sine, *refs):
    pieces = refs[:count]
    turned, top_ref, sum_ref, buffer, blocks, semaphores, block_semaphores = refs[count:]
    group_size, pages_each = blocks.shape[0], blocks.shape[1]
    slice_index = meta[1]

    def block_copy(relative):
        piece, index = extension_at(relative)
        return pltpu.make_async_copy(
            pieces[piece].at[pl.ds(index, pages_each)],
            blocks.at[relative],
            block_semaphores.at[relative],
        )

    for relative in range(group_size):
        block_copy(relative).start()
    found = start_pages(
        reuse, 1, functools.partial(place, slots, meta), pieces, buffer, semaphores
    )
    scale = HEAD_DIM**-0.5
    cos_rows, sin_rows = cosine[...], sine[...]
    for group in range(GQ):
        values = query[:, group * HEAD_DIM : (group + 1) * HEAD_DIM].astype(jnp.float32)
        rotated = values * cos_rows + pltpu.roll(values, HEAD_DIM // 2, 1) * sin_rows
        turned[group] = (rotated * scale).astype(jnp.bfloat16)

    row_count = query.shape[0]
    rows = lax.broadcasted_iota(jnp.int32, (row_count, row_count), 0)
    columns = lax.broadcasted_iota(jnp.int32, (row_count, row_count), 1)

    def attend(index, **options):
        fold(turned, blocks[index].reshape(row_count, PAIR), top_ref, sum_ref, **options)

    for relative in range(group_size):
        block_copy(relative).wait()
    attend(0, mask=columns <= rows, first=True)

    def earlier(index, carry):
        attend(index ^ slice_index)
        return carry

    lax.fori_loop(0, slice_index, earlier, 0)

    def wait_page(index):
        pltpu.make_async_copy(pieces[0].at[0], buffer.at[index], semaphores.at[index]).wait()

    fold_pages(turned, buffer, wait_page, found, top_ref, sum_ref)


def attend_early(
    place, extension_at, group_size, slots, reuse, meta, queries, row_cos, row_sin, pieces
):
    page_count, row_count, page_rows = reuse.shape[0], queries.shape[0], pieces[0].shape[1]
    in_smem = pl.BlockSpec(memory_space=pltpu.SMEM)
    in_vmem = pl.BlockSpec(memory_space=pltpu.VMEM)
    anywhere = pl.BlockSpec(memory_space=pl.ANY)
    shape = (GQ, row_count, HEAD_DIM)
    work = GQ * row_count * page_count * page_rows
    return pl.pallas_call(
        functools.partial(early_kernel, place, extension_at, len(pieces), slots),
        in_specs=[in_smem] * 2 + [in_vmem] * 3 + [anywhere] * len(pieces),
        out_specs=[in_vmem] * 3,
        out_shape=[
            jax.ShapeDtypeStruct(shape, jnp.bfloat16),
            jax.ShapeDtypeStruct(shape, jnp.float32),
            jax.ShapeDtypeStruct((GQ, row_count, PAIR), jnp.float32),
        ],
        scratch_shapes=[
            pltpu.VMEM((page_count, page_rows, PAIR), jnp.bfloat16),
            pltpu.VMEM((group_size, row_count // page_rows, page_rows, PAIR), jnp.bfloat16),
            pltpu.SemaphoreType.DMA((page_count,)),
            pltpu.SemaphoreType.DMA((group_size,)),
        ],
        compiler_params=pltpu.CompilerParams(vmem_limit_bytes=24 << 20),
        cost_estimate=pl.CostEstimate(
            flops=4 * work * HEAD_DIM,
            bytes_accessed=page_rows * page_count * PAIR * 2,
            transcendentals=work,
        ),
        name="early",
    )(reuse, meta, queries, row_cos, row_sin, *pieces)


def place_spread(group_size, slots, meta, slot):
    device = slot // slots
    return meta[1] ^ (device % group_size), device // group_size * slots + slot % slots


def place_apart(slots, meta, slot):
    device = slot // slots
    source, relative = device // 4, meta[1] ^ (device % 4)
    shift = (meta[0] - source) & 3
    return (relative & 1) * 6 + (shift ^ (shift >> 1)), (relative >> 1) * slots + slot % slots


def fresh_place(group_size, meta, device):
    source, spot = device // group_size, device % group_size
    holder = (spot - (spot & 1)) + (source & 1)
    index = ((source >> 1) ^ meta[2]) * 2 + ((spot ^ (meta[0] >> 1)) & 1)
    return meta[1] ^ holder, index


def late_kernel(group_size, reuse, meta, turned, top_in, sum_in, *refs):
    pieces = refs[:group_size]
    out, top_ref, sum_ref, buffer, semaphores = refs[group_size:]
    place = functools.partial(fresh_place, group_size, meta)
    count = start_pages(reuse, 0, place, pieces, buffer, semaphores)
    top_ref[...] = jnp.full_like(top_ref, MASK_VALUE)
    sum_ref[...] = jnp.zeros_like(sum_ref)

    def wait_page(index):
        pltpu.make_async_copy(pieces[0].at[0], buffer.at[index], semaphores.at[index]).wait()

    fold_pages(turned, buffer, wait_page, count, top_ref, sum_ref)
    for group in range(GQ):
        first_top, last_top = top_in[group], top_ref[group]
        row_top = jnp.maximum(first_top, last_top)
        first_share, last_share = jnp.exp(first_top - row_top), jnp.exp(last_top - row_top)
        total = sum_in[group] * jnp.concatenate([first_share, first_share], axis=1)
        total += sum_ref[group] * jnp.concatenate([last_share, last_share], axis=1)
        out[:, group * HEAD_DIM : (group + 1) * HEAD_DIM] = (
            total[:, :HEAD_DIM] / total[:, HEAD_DIM:]
        ).astype(out.dtype)


def attend_late(reuse, meta, turned, top, total, pieces):
    page_count, row_count, page_rows = reuse.shape[0], turned.shape[1], pieces[0].shape[1]
    group_size = len(pieces)
    most = min(page_count, group_size * pieces[0].shape[0])
    in_smem = pl.BlockSpec(memory_space=pltpu.SMEM)
    in_vmem = pl.BlockSpec(memory_space=pltpu.VMEM)
    anywhere = pl.BlockSpec(memory_space=pl.ANY)
    work = GQ * row_count * page_rows * page_count // 2
    return pl.pallas_call(
        functools.partial(late_kernel, group_size),
        in_specs=[in_smem] * 2 + [in_vmem] * 3 + [anywhere] * group_size,
        out_specs=in_vmem,
        out_shape=jax.ShapeDtypeStruct((row_count, GQ * HEAD_DIM), jnp.bfloat16),
        scratch_shapes=[
            pltpu.VMEM(top.shape, top.dtype),
            pltpu.VMEM(total.shape, total.dtype),
            pltpu.VMEM((most, page_rows, PAIR), jnp.bfloat16),
            pltpu.SemaphoreType.DMA((most,)),
        ],
        compiler_params=pltpu.CompilerParams(vmem_limit_bytes=24 << 20),
        cost_estimate=pl.CostEstimate(
            flops=4 * work * HEAD_DIM,
            bytes_accessed=page_rows * page_count * PAIR,
            transcendentals=work,
        ),
        name="late",
    )(reuse, meta, turned, top, total, *pieces)


def on_device(parts, queries, ext_kv, page_store, prefix_hidden, kv_weight, kv_bias, reuse):
    devices = lax.axis_size("kv")
    own_index = lax.axis_index("kv")
    part_index = lax.axis_index("grp")
    row_count = queries.shape[0]
    group_size = devices // HEADS
    group_bits = group_size.bit_length() - 1
    head = own_index >> group_bits
    slice_index = own_index & (group_size - 1)
    core = own_index & 1
    side = part_index & 1
    page_count = reuse.shape[0]
    slots, page_rows = page_store.shape[0], page_store.shape[1]

    def exchange(value, bit):
        return swap(value, "kv", bit, devices)

    def between_planes(value):
        groups = [list(range(spot, devices, group_size)) for spot in range(group_size)]
        return lax.all_to_all(value, "kv", 0, 0, axis_index_groups=groups, tiled=True)

    hidden_across = swap(prefix_hidden, "grp", 1, parts)

    target = 2 * core + side
    spare = 2 * (1 - core) + side
    mine = lax.dynamic_slice_in_dim(kv_weight, target * PAIR, PAIR, 1)
    other = exchange(lax.dynamic_slice_in_dim(kv_weight, spare * PAIR, PAIR, 1), 1)
    chip_rows = jnp.where(
        core == 0,
        jnp.concatenate([mine, other], axis=0),
        jnp.concatenate([other, mine], axis=0),
    )

    def as_pages(*blocks):
        return jnp.concatenate(blocks, axis=0).reshape(-1, page_rows, PAIR)

    def stored_for(store, plane):
        part = lax.dynamic_slice_in_dim(store, plane * PAIR, PAIR, 2)
        return part.reshape(slots * page_rows, PAIR)

    order = []
    if group_size == 4:
        def to_plane(value, shift):
            step = shift * group_size
            return lax.ppermute(value, "kv", [(i, (i + step) % devices) for i in range(devices)])

        near, back = to_plane(chip_rows, 1), to_plane(chip_rows, 3)
        beside_own = exchange(chip_rows, 2)
        store_beside = exchange(page_store, 2)
        far = to_plane(near, 1)
        near_sent, _ = lax.optimization_barrier((near, beside_own))
        beside_near = exchange(near_sent, 2)
        back_sent, store_beside, _ = lax.optimization_barrier((back, store_beside, beside_near))
        beside_back = exchange(back_sent, 2)
        far_sent, hidden_mine, hidden_passed, reuse_sent, stores, _ = lax.optimization_barrier(
            (far, prefix_hidden, hidden_across, reuse, (page_store, store_beside), beside_back)
        )
        hidden_core = exchange(hidden_mine, 1)
        beside_far = exchange(far_sent, 2)
        def parts_for(shift):
            return as_pages(*[stored_for(store, (head + shift) & (HEADS - 1)) for store in stores])

        others = [
            lax.ppermute(
                parts_for(shift),
                "kv",
                [(i, (i + shift * group_size) % devices) for i in range(devices)],
            )
            for shift in (1, 3, 2)
        ]
        own_parts = parts_for(0)
        weights = [chip_rows, beside_own, near, beside_near, back, beside_back, far, beside_far]
        for shift in (0, 1, 3, 2):
            chip = (((head - shift) & (HEADS - 1)) << 1) | (slice_index >> 1)
            order += [chip, chip ^ 1]
    else:
        hidden_core, hidden_passed, reuse_sent = exchange(prefix_hidden, 1), hidden_across, reuse
        weights = [
            lax.all_gather(
                chip_rows,
                "kv",
                axis=0,
                tiled=True,
                axis_index_groups=[list(range(first, devices, 2)) for first in range(2)],
            )
        ]
    hidden_diagonal = exchange(hidden_passed, 1)
    reuse_across = swap(reuse_sent, "grp", 1, parts)
    offset = page_count * page_rows
    (ext_kv, first_row), _ = lax.optimization_barrier(
        ((ext_kv, slice_index * row_count), weights[min(2, len(weights) - 1)])
    )
    query_pos = offset + first_row + jnp.arange(row_count, dtype=jnp.int32)
    row_cos, row_sin = angle_tables(query_pos)
    raw_keys = ext_kv[:, :HEAD_DIM].astype(jnp.float32)
    own_keys = raw_keys * row_cos + jnp.roll(raw_keys, HEAD_DIM // 2, axis=1) * row_sin
    own_block = jnp.concatenate([own_keys.astype(jnp.bfloat16), ext_kv[:, HEAD_DIM:]], axis=1)

    if group_size == 4:
        own_sent, _ = lax.optimization_barrier((own_block, weights[5]))
        block_beside = as_pages(exchange(own_sent, 2))
        own_pages = as_pages(own_block)
        own_cores = [exchange(own_parts, 1), exchange(own_pages, 1)]

    def page_numbers(table):
        match = (table[:, 0] == 0)[:, None] & (
            table[:, 2][:, None] == jnp.stack([own_index, own_index ^ 1])[None, :]
        )
        return jnp.sum(
            jnp.where(match, jnp.arange(page_count, dtype=jnp.int32)[:, None], 0), axis=0
        )

    numbers = jnp.concatenate([page_numbers(reuse), page_numbers(reuse_across)])
    page_cos, page_sin = angle_tables(
        numbers[:, None] * page_rows + jnp.arange(page_rows, dtype=jnp.int32)[None, :]
    )

    bias = lax.dynamic_slice_in_dim(kv_bias, target * PAIR, PAIR, 0).astype(jnp.float32)[None, :]
    first_side = (head >> 1) ^ side
    choice = jnp.stack([first_side, first_side ^ 1] + order).astype(jnp.int32)
    messages = project(
        choice,
        (prefix_hidden, hidden_core, hidden_across, hidden_diagonal),
        weights,
        bias,
        page_cos,
        page_sin,
    )
    received = []
    for turn, message in enumerate(messages):
        routes = []
        for part in range(parts):
            for device in range(devices):
                plane, spot = device // group_size, device % group_size
                to_part = (part & ~1) | ((plane >> 1) ^ turn)
                to_spot = (spot & ~1) | (plane & 1)
                to_head = 2 * (spot & 1) + (part & 1)
                routes.append(
                    (part * devices + device, to_part * devices + to_head * group_size + to_spot)
                )
        received.append(lax.ppermute(message, ("grp", "kv"), routes))
    meta = jnp.stack([head, slice_index, side]).astype(jnp.int32)
    bits = []
    while 1 << len(bits) < group_size:
        bits.insert(0, 1 << len(bits))

    def spread(own, first):
        pieces = {0: own, bits[0]: first}
        for bit in bits[1:]:
            pieces.update({known ^ bit: exchange(value, bit) for known, value in pieces.items()})
        return [pieces[relative] for relative in range(group_size)]

    if group_size == 4:
        others, block_beside = lax.optimization_barrier(
            ((others, block_beside), received)
        )[0]
        pieces = [own_parts, *others, own_pages, block_beside]
        pieces += [
            own_cores[0],
            *[exchange(piece, 1) for piece in others],
            own_cores[1],
            exchange(block_beside, 1),
        ]
        place = place_apart
        extension_at = lambda relative: ((relative & 1) * 6 + 4 + (relative >> 1), 0)
    else:
        per_head = page_store.reshape(slots, page_rows, HEADS, PAIR).transpose(2, 0, 1, 3)
        arrived = between_planes(per_head.reshape(HEADS * slots, page_rows, PAIR))
        gathered = as_pages(arrived.reshape(-1, PAIR), own_block)
        pieces = spread(gathered, exchange(gathered, bits[0]))
        place = functools.partial(place_spread, group_size)
        extension_at = lambda relative: (relative, HEADS * slots)
    turned, top, total = attend_early(
        place, extension_at, group_size, slots, reuse, meta, queries, row_cos, row_sin, pieces
    )
    late_own = jnp.concatenate(received, axis=0)
    late_first = exchange(late_own, bits[0])
    late_first, turned = lax.optimization_barrier((late_first, turned))
    late_pieces = spread(late_own, late_first)
    return attend_late(reuse, meta, turned, top, total, late_pieces)


def solution(mesh):
    placed = (
        P(("grp", "kv"), None),
        P(("grp", "kv"), None),
        P(("grp", "kv"), None, None),
        P(("grp", "kv"), None, None),
        P("kv", None),
        P(),
        P("grp", None),
    )
    return jax.shard_map(
        functools.partial(on_device, mesh.shape["grp"]),
        mesh=mesh,
        in_specs=placed,
        out_specs=P(("grp", "kv"), None),
        check_vma=False,
    )
```

```python
import functools

import jax
import jax.numpy as jnp
from jax import lax
from jax.experimental import pallas as pl
from jax.experimental.pallas import tpu as pltpu
from jax.sharding import PartitionSpec as P

GQ = 5
HEAD_DIM = 128
PAIR = 2 * HEAD_DIM
HEADS = 4
ONES = 16

ROPE_BASE = 1000000.0
MASK_VALUE = -1e30


def swap(value, axis, bit, count):
    return lax.ppermute(value, axis, [(i, i ^ bit) for i in range(count)])


def angle_tables(positions):
    half_dim = HEAD_DIM // 2
    frequency = ROPE_BASE ** (-jnp.arange(half_dim, dtype=jnp.float32) * 2.0 / HEAD_DIM)
    angles = positions.astype(jnp.float32)[..., None] * frequency
    cosine = jnp.cos(angles)
    sine = jnp.sin(angles)
    return (
        jnp.concatenate([cosine, cosine], axis=-1),
        jnp.concatenate([-sine, sine], axis=-1),
    )


def project_kernel(blocks, meta, *refs):
    pages, weights = refs[:4], refs[4:-6]
    bias, cosine, sine, out_first, out_second, total = refs[-6:]
    rows = cosine.shape[1]
    span = pages[0].shape[2] // blocks
    single = len(weights) == 1

    for block in range(blocks):
        chip = block if single else meta[2 + block]
        start = pl.multiple_of(chip * span, HEAD_DIM)
        left = jnp.concatenate([page[0, :, pl.ds(start, span)] for page in pages], axis=0)
        right = weights[0][pl.ds(block * span, span)] if single else weights[block][...]
        product = jnp.dot(left, right, preferred_element_type=jnp.float32)
        total[...] = product + (bias[...] if block == 0 else total[...])
    for out, place in ((out_first, 0), (out_second, 1)):
        base = meta[place] * 2
        for rel in range(2):
            page = total[pl.ds(pl.multiple_of((base + rel) * rows, rows), rows)]
            keys = page[:, :HEAD_DIM]
            turned = keys * cosine[base + rel] + pltpu.roll(keys, HEAD_DIM // 2, 1) * sine[
                base + rel
            ]
            out[rel, :, :HEAD_DIM] = turned.astype(jnp.bfloat16)
            out[rel, :, HEAD_DIM:] = page[:, HEAD_DIM:].astype(jnp.bfloat16)


def project(meta, pages, weights, bias, cosine, sine):
    rows, depth = pages[0].shape[1:]
    width = weights[0].shape[1]
    in_smem = pl.BlockSpec(memory_space=pltpu.SMEM)
    in_vmem = pl.BlockSpec(memory_space=pltpu.VMEM)
    return pl.pallas_call(
        functools.partial(project_kernel, 8),
        in_specs=[in_smem] + [in_vmem] * (4 + len(weights) + 3),
        out_specs=[in_vmem] * 2,
        out_shape=[jax.ShapeDtypeStruct((2, rows, width), jnp.bfloat16)] * 2,
        scratch_shapes=[pltpu.VMEM((4 * rows, width), jnp.float32)],
        compiler_params=pltpu.CompilerParams(vmem_limit_bytes=24 << 20),
        cost_estimate=pl.CostEstimate(
            flops=2 * 4 * rows * depth * width,
            bytes_accessed=2 * (4 * rows + width) * depth,
            transcendentals=0,
        ),
        name="project",
    )(meta, *pages, *weights, bias, cosine, sine)


def fold(query_ref, rows, top_ref, sum_ref, mask=None, first=False):
    key_rows, value_rows = rows[:, :HEAD_DIM], rows[:, HEAD_DIM:]
    values = value_rows.astype(jnp.float32).T.astype(jnp.bfloat16)
    extended = jnp.concatenate([values, jnp.ones((ONES, rows.shape[0]), jnp.bfloat16)], axis=0)

    def scores_of(group):
        scores = lax.dot_general(
            key_rows,
            query_ref[group],
            (((1,), (1,)), ((), ())),
            preferred_element_type=jnp.float32,
        )
        return scores if mask is None else jnp.where(mask, scores, MASK_VALUE)

    ahead = scores_of(0)
    for group in range(GQ):
        scores = ahead
        if group + 1 < GQ:
            ahead = scores_of(group + 1)
        top = jnp.max(scores, axis=0, keepdims=True)
        if not first:
            old_top = top_ref[group]
            top = jnp.maximum(old_top, top)
        weights = jnp.exp(scores - top).astype(jnp.bfloat16)
        product = jnp.dot(extended, weights, preferred_element_type=jnp.float32)
        if not first:
            product += sum_ref[group] * jnp.exp(old_top - top)
        sum_ref[group] = product
        top_ref[group] = top


def fold_pages(query_ref, buffer, wait_page, count, top_ref, sum_ref):
    def part(start, size):
        for offset in range(size):
            wait_page(start + offset)
        rows = buffer[pl.ds(start, size)].reshape(size * buffer.shape[1], PAIR)
        fold(query_ref, rows, top_ref, sum_ref)

    full = count // 4

    def body(index, carry):
        part(index * 4, 4)
        return carry

    lax.fori_loop(0, full, body, 0)

    @pl.when((count & 2) != 0)
    def _():
        part(full * 4, 2)

    @pl.when((count & 1) != 0)
    def _():
        part(count - 1, 1)


def start_pages(reuse, flag, place, pieces, buffer, semaphores):
    page_count = reuse.shape[0]

    def body(page, count):
        chosen = reuse[page, 0] == flag

        @pl.when(chosen)
        def _():
            piece, index = place(reuse[page, 2 - flag])
            for number, source in enumerate(pieces):

                @pl.when(piece == number)
                def _():
                    pltpu.make_async_copy(
                        source.at[index], buffer.at[count], semaphores.at[count]
                    ).start()

        return count + chosen.astype(jnp.int32)

    return lax.fori_loop(0, page_count, body, jnp.int32(0))


def early_kernel(place, extension_at, count, slots, reuse, meta, query, cosine, sine, *refs):
    pieces = refs[:count]
    turned, top_ref, sum_ref, buffer, blocks, semaphores, block_semaphores = refs[count:]
    group_size, pages_each = blocks.shape[0], blocks.shape[1]
    slice_index = meta[1]

    def block_copy(relative):
        piece, index = extension_at(relative)
        return pltpu.make_async_copy(
            pieces[piece].at[pl.ds(index, pages_each)],
            blocks.at[relative],
            block_semaphores.at[relative],
        )

    for relative in range(group_size):
        block_copy(relative).start()
    found = start_pages(
        reuse, 1, functools.partial(place, slots, meta), pieces, buffer, semaphores
    )
    scale = HEAD_DIM**-0.5
    cos_rows, sin_rows = cosine[...], sine[...]
    for group in range(GQ):
        values = query[:, group * HEAD_DIM : (group + 1) * HEAD_DIM].astype(jnp.float32)
        rotated = values * cos_rows + pltpu.roll(values, HEAD_DIM // 2, 1) * sin_rows
        turned[group] = (rotated * scale).astype(jnp.bfloat16)

    row_count = query.shape[0]
    rows = lax.broadcasted_iota(jnp.int32, (row_count, row_count), 0)
    columns = lax.broadcasted_iota(jnp.int32, (row_count, row_count), 1)

    def attend(index, **options):
        fold(turned, blocks[index].reshape(row_count, PAIR), top_ref, sum_ref, **options)

    for relative in range(group_size):
        block_copy(relative).wait()
    attend(0, mask=rows <= columns, first=True)

    def earlier(index, carry):
        attend(index ^ slice_index)
        return carry

    lax.fori_loop(0, slice_index, earlier, 0)

    def wait_page(index):
        pltpu.make_async_copy(pieces[0].at[0], buffer.at[index], semaphores.at[index]).wait()

    fold_pages(turned, buffer, wait_page, found, top_ref, sum_ref)


def attend_early(
    place, extension_at, group_size, slots, reuse, meta, queries, row_cos, row_sin, pieces
):
    page_count, row_count, page_rows = reuse.shape[0], queries.shape[0], pieces[0].shape[1]
    in_smem = pl.BlockSpec(memory_space=pltpu.SMEM)
    in_vmem = pl.BlockSpec(memory_space=pltpu.VMEM)
    anywhere = pl.BlockSpec(memory_space=pl.ANY)
    shape = (GQ, row_count, HEAD_DIM)
    work = GQ * row_count * page_count * page_rows
    return pl.pallas_call(
        functools.partial(early_kernel, place, extension_at, len(pieces), slots),
        in_specs=[in_smem] * 2 + [in_vmem] * 3 + [anywhere] * len(pieces),
        out_specs=[in_vmem] * 3,
        out_shape=[
            jax.ShapeDtypeStruct(shape, jnp.bfloat16),
            jax.ShapeDtypeStruct((GQ, 1, row_count), jnp.float32),
            jax.ShapeDtypeStruct((GQ, HEAD_DIM + ONES, row_count), jnp.float32),
        ],
        scratch_shapes=[
            pltpu.VMEM((page_count, page_rows, PAIR), jnp.bfloat16),
            pltpu.VMEM((group_size, row_count // page_rows, page_rows, PAIR), jnp.bfloat16),
            pltpu.SemaphoreType.DMA((page_count,)),
            pltpu.SemaphoreType.DMA((group_size,)),
        ],
        compiler_params=pltpu.CompilerParams(vmem_limit_bytes=24 << 20),
        cost_estimate=pl.CostEstimate(
            flops=4 * work * HEAD_DIM,
            bytes_accessed=page_rows * page_count * PAIR * 2,
            transcendentals=work,
        ),
        name="early",
    )(reuse, meta, queries, row_cos, row_sin, *pieces)


def place_spread(group_size, slots, meta, slot):
    device = slot // slots
    return meta[1] ^ (device % group_size), device // group_size * slots + slot % slots


def place_apart(slots, meta, slot):
    device = slot // slots
    source, relative = device // 4, meta[1] ^ (device % 4)
    shift = (meta[0] - source) & 3
    return (relative & 1) * 6 + (shift ^ (shift >> 1)), (relative >> 1) * slots + slot % slots


def fresh_place(group_size, meta, device):
    source, spot = device // group_size, device % group_size
    holder = (spot - (spot & 1)) + (source & 1)
    index = ((source >> 1) ^ meta[2]) * 2 + ((spot ^ (meta[0] >> 1)) & 1)
    return meta[1] ^ holder, index


def late_kernel(group_size, reuse, meta, turned, top_in, sum_in, *refs):
    pieces = refs[:group_size]
    out, top_ref, sum_ref, buffer, semaphores = refs[group_size:]
    place = functools.partial(fresh_place, group_size, meta)
    count = start_pages(reuse, 0, place, pieces, buffer, semaphores)
    top_ref[...] = jnp.full_like(top_ref, MASK_VALUE)
    sum_ref[...] = jnp.zeros_like(sum_ref)

    def wait_page(index):
        pltpu.make_async_copy(pieces[0].at[0], buffer.at[index], semaphores.at[index]).wait()

    fold_pages(turned, buffer, wait_page, count, top_ref, sum_ref)
    for group in range(GQ):
        first_top, last_top = top_in[group], top_ref[group]
        top = jnp.maximum(first_top, last_top)
        total = sum_in[group] * jnp.exp(first_top - top)
        total += sum_ref[group] * jnp.exp(last_top - top)
        result = total[:HEAD_DIM] / total[HEAD_DIM : HEAD_DIM + 1]
        out[:, group * HEAD_DIM : (group + 1) * HEAD_DIM] = result.T.astype(out.dtype)


def attend_late(reuse, meta, turned, top, total, pieces):
    page_count, row_count, page_rows = reuse.shape[0], turned.shape[1], pieces[0].shape[1]
    group_size = len(pieces)
    most = min(page_count, group_size * pieces[0].shape[0])
    in_smem = pl.BlockSpec(memory_space=pltpu.SMEM)
    in_vmem = pl.BlockSpec(memory_space=pltpu.VMEM)
    anywhere = pl.BlockSpec(memory_space=pl.ANY)
    work = GQ * row_count * page_rows * page_count // 2
    return pl.pallas_call(
        functools.partial(late_kernel, group_size),
        in_specs=[in_smem] * 2 + [in_vmem] * 3 + [anywhere] * group_size,
        out_specs=in_vmem,
        out_shape=jax.ShapeDtypeStruct((row_count, GQ * HEAD_DIM), jnp.bfloat16),
        scratch_shapes=[
            pltpu.VMEM(top.shape, top.dtype),
            pltpu.VMEM(total.shape, total.dtype),
            pltpu.VMEM((most, page_rows, PAIR), jnp.bfloat16),
            pltpu.SemaphoreType.DMA((most,)),
        ],
        compiler_params=pltpu.CompilerParams(vmem_limit_bytes=24 << 20),
        cost_estimate=pl.CostEstimate(
            flops=4 * work * HEAD_DIM,
            bytes_accessed=page_rows * page_count * PAIR,
            transcendentals=work,
        ),
        name="late",
    )(reuse, meta, turned, top, total, *pieces)


def on_device(parts, queries, ext_kv, page_store, prefix_hidden, kv_weight, kv_bias, reuse):
    devices = lax.axis_size("kv")
    own_index = lax.axis_index("kv")
    part_index = lax.axis_index("grp")
    row_count = queries.shape[0]
    group_size = devices // HEADS
    group_bits = group_size.bit_length() - 1
    head = own_index >> group_bits
    slice_index = own_index & (group_size - 1)
    core = own_index & 1
    side = part_index & 1
    page_count = reuse.shape[0]
    slots, page_rows = page_store.shape[0], page_store.shape[1]

    def exchange(value, bit):
        return swap(value, "kv", bit, devices)

    def between_planes(value):
        groups = [list(range(spot, devices, group_size)) for spot in range(group_size)]
        return lax.all_to_all(value, "kv", 0, 0, axis_index_groups=groups, tiled=True)

    hidden_across = swap(prefix_hidden, "grp", 1, parts)

    target = 2 * core + side
    spare = 2 * (1 - core) + side
    mine = lax.dynamic_slice_in_dim(kv_weight, target * PAIR, PAIR, 1)
    other = exchange(lax.dynamic_slice_in_dim(kv_weight, spare * PAIR, PAIR, 1), 1)
    chip_rows = jnp.where(
        core == 0,
        jnp.concatenate([mine, other], axis=0),
        jnp.concatenate([other, mine], axis=0),
    )

    def as_pages(*blocks):
        return jnp.concatenate(blocks, axis=0).reshape(-1, page_rows, PAIR)

    def stored_for(store, plane):
        part = lax.dynamic_slice_in_dim(store, plane * PAIR, PAIR, 2)
        return part.reshape(slots * page_rows, PAIR)

    order = []
    if group_size == 4:
        def to_plane(value, shift):
            step = shift * group_size
            return lax.ppermute(value, "kv", [(i, (i + step) % devices) for i in range(devices)])

        near, back = to_plane(chip_rows, 1), to_plane(chip_rows, 3)
        beside_own = exchange(chip_rows, 2)
        store_beside = exchange(lax.optimization_barrier((page_store, chip_rows))[0], 2)
        far = to_plane(near, 1)
        near_sent, _ = lax.optimization_barrier((near, beside_own))
        beside_near = exchange(near_sent, 2)
        back_sent, store_beside, _ = lax.optimization_barrier((back, store_beside, beside_near))
        beside_back = exchange(back_sent, 2)
        far_sent, hidden_mine, hidden_passed, reuse_sent, stores, _ = lax.optimization_barrier(
            (far, prefix_hidden, hidden_across, reuse, (page_store, store_beside), beside_back)
        )
        hidden_core = exchange(hidden_mine, 1)
        beside_far = exchange(far_sent, 2)
        def parts_for(shift):
            return as_pages(*[stored_for(store, (head + shift) & (HEADS - 1)) for store in stores])

        others = [
            lax.ppermute(
                parts_for(shift),
                "kv",
                [(i, (i + shift * group_size) % devices) for i in range(devices)],
            )
            for shift in (1, 3, 2)
        ]
        own_parts = parts_for(0)
        weights = [chip_rows, beside_own, near, beside_near, back, beside_back, far, beside_far]
        for shift in (0, 1, 3, 2):
            chip = (((head - shift) & (HEADS - 1)) << 1) | (slice_index >> 1)
            order += [chip, chip ^ 1]
    else:
        hidden_core, hidden_passed, reuse_sent = exchange(prefix_hidden, 1), hidden_across, reuse
        weights = [
            lax.all_gather(
                chip_rows,
                "kv",
                axis=0,
                tiled=True,
                axis_index_groups=[list(range(first, devices, 2)) for first in range(2)],
            )
        ]
    hidden_diagonal = exchange(hidden_passed, 1)
    reuse_across = swap(reuse_sent, "grp", 1, parts)
    offset = page_count * page_rows
    (ext_kv, first_row), _ = lax.optimization_barrier(
        ((ext_kv, slice_index * row_count), weights[min(2, len(weights) - 1)])
    )
    query_pos = offset + first_row + jnp.arange(row_count, dtype=jnp.int32)
    row_cos, row_sin = angle_tables(query_pos)
    raw_keys = ext_kv[:, :HEAD_DIM].astype(jnp.float32)
    own_keys = raw_keys * row_cos + jnp.roll(raw_keys, HEAD_DIM // 2, axis=1) * row_sin
    own_block = jnp.concatenate([own_keys.astype(jnp.bfloat16), ext_kv[:, HEAD_DIM:]], axis=1)

    if group_size == 4:
        own_sent, _ = lax.optimization_barrier((own_block, weights[5]))
        block_beside = as_pages(exchange(own_sent, 2))
        own_pages = as_pages(own_block)
        own_cores = [exchange(own_parts, 1), exchange(own_pages, 1)]

    def page_numbers(table):
        match = (table[:, 0] == 0)[:, None] & (
            table[:, 2][:, None] == jnp.stack([own_index, own_index ^ 1])[None, :]
        )
        return jnp.sum(
            jnp.where(match, jnp.arange(page_count, dtype=jnp.int32)[:, None], 0), axis=0
        )

    numbers = jnp.concatenate([page_numbers(reuse), page_numbers(reuse_across)])
    page_cos, page_sin = angle_tables(
        numbers[:, None] * page_rows + jnp.arange(page_rows, dtype=jnp.int32)[None, :]
    )

    bias = lax.dynamic_slice_in_dim(kv_bias, target * PAIR, PAIR, 0).astype(jnp.float32)[None, :]
    first_side = (head >> 1) ^ side
    choice = jnp.stack([first_side, first_side ^ 1] + order).astype(jnp.int32)
    messages = project(
        choice,
        (prefix_hidden, hidden_core, hidden_across, hidden_diagonal),
        weights,
        bias,
        page_cos,
        page_sin,
    )
    received = []
    for turn, message in enumerate(messages):
        routes = []
        for part in range(parts):
            for device in range(devices):
                plane, spot = device // group_size, device % group_size
                to_part = (part & ~1) | ((plane >> 1) ^ turn)
                to_spot = (spot & ~1) | (plane & 1)
                to_head = 2 * (spot & 1) + (part & 1)
                routes.append(
                    (part * devices + device, to_part * devices + to_head * group_size + to_spot)
                )
        received.append(lax.ppermute(message, ("grp", "kv"), routes))
    meta = jnp.stack([head, slice_index, side]).astype(jnp.int32)
    bits = []
    while 1 << len(bits) < group_size:
        bits.insert(0, 1 << len(bits))

    def spread(own, first):
        pieces = {0: own, bits[0]: first}
        for bit in bits[1:]:
            pieces.update({known ^ bit: exchange(value, bit) for known, value in pieces.items()})
        return [pieces[relative] for relative in range(group_size)]

    if group_size == 4:
        others, block_beside = lax.optimization_barrier(
            ((others, block_beside), received)
        )[0]
        pieces = [own_parts, *others, own_pages, block_beside]
        pieces += [
            own_cores[0],
            *[exchange(piece, 1) for piece in others],
            own_cores[1],
            exchange(block_beside, 1),
        ]
        place = place_apart
        extension_at = lambda relative: ((relative & 1) * 6 + 4 + (relative >> 1), 0)
    else:
        per_head = page_store.reshape(slots, page_rows, HEADS, PAIR).transpose(2, 0, 1, 3)
        arrived = between_planes(per_head.reshape(HEADS * slots, page_rows, PAIR))
        gathered = as_pages(arrived.reshape(-1, PAIR), own_block)
        pieces = spread(gathered, exchange(gathered, bits[0]))
        place = functools.partial(place_spread, group_size)
        extension_at = lambda relative: (relative, HEADS * slots)
    turned, top, total = attend_early(
        place, extension_at, group_size, slots, reuse, meta, queries, row_cos, row_sin, pieces
    )
    late_own = jnp.concatenate(received, axis=0)
    late_first = exchange(late_own, bits[0])
    late_first, turned = lax.optimization_barrier((late_first, turned))
    late_pieces = spread(late_own, late_first)
    return attend_late(reuse, meta, turned, top, total, late_pieces)


def solution(mesh):
    placed = (
        P(("grp", "kv"), None),
        P(("grp", "kv"), None),
        P(("grp", "kv"), None, None),
        P(("grp", "kv"), None, None),
        P("kv", None),
        P(),
        P("grp", None),
    )
    return jax.shard_map(
        functools.partial(on_device, mesh.shape["grp"]),
        mesh=mesh,
        in_specs=placed,
        out_specs=P(("grp", "kv"), None),
        check_vma=False,
    )
```

```python
import functools

import jax
import jax.numpy as jnp
from jax import lax
from jax.experimental import pallas as pl
from jax.experimental.pallas import tpu as pltpu
from jax.sharding import PartitionSpec as P

GQ = 5
HEAD_DIM = 128
PAIR = 2 * HEAD_DIM
HEADS = 4

ROPE_BASE = 1000000.0
MASK_VALUE = -1e30


def swap(value, axis, bit, count):
    return lax.ppermute(value, axis, [(i, i ^ bit) for i in range(count)])


def angle_tables(positions):
    half_dim = HEAD_DIM // 2
    frequency = ROPE_BASE ** (-jnp.arange(half_dim, dtype=jnp.float32) * 2.0 / HEAD_DIM)
    angles = positions.astype(jnp.float32)[..., None] * frequency
    cosine = jnp.cos(angles)
    sine = jnp.sin(angles)
    return (
        jnp.concatenate([cosine, cosine], axis=-1),
        jnp.concatenate([-sine, sine], axis=-1),
    )


def project_kernel(blocks, meta, *refs):
    pages, weights = refs[:4], refs[4:-6]
    bias, cosine, sine, out_first, out_second, total = refs[-6:]
    rows = cosine.shape[1]
    span = pages[0].shape[2] // blocks
    single = len(weights) == 1

    for block in range(blocks):
        chip = block if single else meta[2 + block]
        start = pl.multiple_of(chip * span, HEAD_DIM)
        left = jnp.concatenate([page[0, :, pl.ds(start, span)] for page in pages], axis=0)
        right = weights[0][pl.ds(block * span, span)] if single else weights[block][...]
        product = jnp.dot(left, right, preferred_element_type=jnp.float32)
        total[...] = product + (bias[...] if block == 0 else total[...])
    for out, place in ((out_first, 0), (out_second, 1)):
        base = meta[place] * 2
        for rel in range(2):
            page = total[pl.ds(pl.multiple_of((base + rel) * rows, rows), rows)]
            keys = page[:, :HEAD_DIM]
            turned = keys * cosine[base + rel] + pltpu.roll(keys, HEAD_DIM // 2, 1) * sine[
                base + rel
            ]
            out[rel, :, :HEAD_DIM] = turned.astype(jnp.bfloat16)
            out[rel, :, HEAD_DIM:] = page[:, HEAD_DIM:].astype(jnp.bfloat16)


def project(meta, pages, weights, bias, cosine, sine):
    rows, depth = pages[0].shape[1:]
    width = weights[0].shape[1]
    in_smem = pl.BlockSpec(memory_space=pltpu.SMEM)
    in_vmem = pl.BlockSpec(memory_space=pltpu.VMEM)
    return pl.pallas_call(
        functools.partial(project_kernel, 8),
        in_specs=[in_smem] + [in_vmem] * (4 + len(weights) + 3),
        out_specs=[in_vmem] * 2,
        out_shape=[jax.ShapeDtypeStruct((2, rows, width), jnp.bfloat16)] * 2,
        scratch_shapes=[pltpu.VMEM((4 * rows, width), jnp.float32)],
        compiler_params=pltpu.CompilerParams(vmem_limit_bytes=24 << 20),
        cost_estimate=pl.CostEstimate(
            flops=2 * 4 * rows * depth * width,
            bytes_accessed=2 * (4 * rows + width) * depth,
            transcendentals=0,
        ),
        name="project",
    )(meta, *pages, *weights, bias, cosine, sine)


def fold(query_ref, rows, top_ref, sum_ref, mask=None, first=False):
    key_rows, value_rows = rows[:, :HEAD_DIM], rows[:, HEAD_DIM:]
    copies = rows.shape[0] // HEAD_DIM
    extended = jnp.concatenate([value_rows, jnp.ones_like(value_rows)], axis=1)

    def scores_of(group):
        scores = lax.dot_general(
            query_ref[group],
            key_rows,
            (((1,), (1,)), ((), ())),
            preferred_element_type=jnp.float32,
        )
        return scores if mask is None else jnp.where(mask, scores, MASK_VALUE)

    ahead = scores_of(0)
    for group in range(GQ):
        scores = ahead
        if group + 1 < GQ:
            ahead = scores_of(group + 1)
        row_top = jnp.broadcast_to(
            jnp.max(scores, axis=1, keepdims=True), (scores.shape[0], HEAD_DIM)
        )
        if not first:
            old_top = top_ref[group]
            row_top = jnp.maximum(old_top, row_top)
        below = scores - jnp.concatenate([row_top] * copies, axis=1)
        weights = jnp.exp(below.astype(jnp.bfloat16))
        product = jnp.dot(weights, extended, preferred_element_type=jnp.float32)
        if not first:
            shrink = jnp.exp(old_top - row_top)
            product += sum_ref[group] * jnp.concatenate([shrink, shrink], axis=1)
        sum_ref[group] = product
        top_ref[group] = row_top


def fold_pages(query_ref, buffer, wait_page, count, top_ref, sum_ref):
    def part(start, size):
        for offset in range(size):
            wait_page(start + offset)
        rows = buffer[pl.ds(start, size)].reshape(size * buffer.shape[1], PAIR)
        fold(query_ref, rows, top_ref, sum_ref)

    full = count // 4

    def body(index, carry):
        part(index * 4, 4)
        return carry

    lax.fori_loop(0, full, body, 0)

    @pl.when((count & 2) != 0)
    def _():
        part(full * 4, 2)

    @pl.when((count & 1) != 0)
    def _():
        part(count - 1, 1)


def start_pages(reuse, flag, place, pieces, buffer, semaphores):
    page_count = reuse.shape[0]

    def body(page, count):
        chosen = reuse[page, 0] == flag

        @pl.when(chosen)
        def _():
            piece, index = place(reuse[page, 2 - flag])
            for number, source in enumerate(pieces):

                @pl.when(piece == number)
                def _():
                    pltpu.make_async_copy(
                        source.at[index], buffer.at[count], semaphores.at[count]
                    ).start()

        return count + chosen.astype(jnp.int32)

    return lax.fori_loop(0, page_count, body, jnp.int32(0))


def early_kernel(place, extension_at, count, slots, reuse, meta, query, cosine, sine, *refs):
    pieces = refs[:count]
    turned, top_ref, sum_ref, buffer, blocks, semaphores, block_semaphores = refs[count:]
    group_size, pages_each = blocks.shape[0], blocks.shape[1]
    slice_index = meta[1]

    def block_copy(relative):
        piece, index = extension_at(relative)
        return pltpu.make_async_copy(
            pieces[piece].at[pl.ds(index, pages_each)],
            blocks.at[relative],
            block_semaphores.at[relative],
        )

    for relative in range(group_size):
        block_copy(relative).start()
    found = start_pages(
        reuse, 1, functools.partial(place, slots, meta), pieces, buffer, semaphores
    )
    scale = HEAD_DIM**-0.5
    cos_rows, sin_rows = cosine[...], sine[...]
    for group in range(GQ):
        values = query[:, group * HEAD_DIM : (group + 1) * HEAD_DIM].astype(jnp.float32)
        rotated = values * cos_rows + pltpu.roll(values, HEAD_DIM // 2, 1) * sin_rows
        turned[group] = (rotated * scale).astype(jnp.bfloat16)

    row_count = query.shape[0]
    rows = lax.broadcasted_iota(jnp.int32, (row_count, row_count), 0)
    columns = lax.broadcasted_iota(jnp.int32, (row_count, row_count), 1)

    def attend(index, **options):
        fold(turned, blocks[index].reshape(row_count, PAIR), top_ref, sum_ref, **options)

    for relative in range(group_size):
        block_copy(relative).wait()
    attend(0, mask=columns <= rows, first=True)

    def earlier(index, carry):
        attend(index ^ slice_index)
        return carry

    lax.fori_loop(0, slice_index, earlier, 0)

    def wait_page(index):
        pltpu.make_async_copy(pieces[0].at[0], buffer.at[index], semaphores.at[index]).wait()

    fold_pages(turned, buffer, wait_page, found, top_ref, sum_ref)


def attend_early(
    place, extension_at, group_size, slots, reuse, meta, queries, row_cos, row_sin, pieces
):
    page_count, row_count, page_rows = reuse.shape[0], queries.shape[0], pieces[0].shape[1]
    in_smem = pl.BlockSpec(memory_space=pltpu.SMEM)
    in_vmem = pl.BlockSpec(memory_space=pltpu.VMEM)
    anywhere = pl.BlockSpec(memory_space=pl.ANY)
    shape = (GQ, row_count, HEAD_DIM)
    work = GQ * row_count * page_count * page_rows
    return pl.pallas_call(
        functools.partial(early_kernel, place, extension_at, len(pieces), slots),
        in_specs=[in_smem] * 2 + [in_vmem] * 3 + [anywhere] * len(pieces),
        out_specs=[in_vmem] * 3,
        out_shape=[
            jax.ShapeDtypeStruct(shape, jnp.bfloat16),
            jax.ShapeDtypeStruct(shape, jnp.float32),
            jax.ShapeDtypeStruct((GQ, row_count, PAIR), jnp.float32),
        ],
        scratch_shapes=[
            pltpu.VMEM((page_count, page_rows, PAIR), jnp.bfloat16),
            pltpu.VMEM((group_size, row_count // page_rows, page_rows, PAIR), jnp.bfloat16),
            pltpu.SemaphoreType.DMA((page_count,)),
            pltpu.SemaphoreType.DMA((group_size,)),
        ],
        compiler_params=pltpu.CompilerParams(vmem_limit_bytes=24 << 20),
        cost_estimate=pl.CostEstimate(
            flops=4 * work * HEAD_DIM,
            bytes_accessed=page_rows * page_count * PAIR * 2,
            transcendentals=work,
        ),
        name="early",
    )(reuse, meta, queries, row_cos, row_sin, *pieces)


def place_spread(group_size, slots, meta, slot):
    device = slot // slots
    return meta[1] ^ (device % group_size), device // group_size * slots + slot % slots


def place_apart(slots, meta, slot):
    device = slot // slots
    source, relative = device // 4, meta[1] ^ (device % 4)
    shift = (meta[0] - source) & 3
    return (relative & 1) * 6 + (shift ^ (shift >> 1)), (relative >> 1) * slots + slot % slots


def fresh_place(group_size, meta, device):
    source, spot = device // group_size, device % group_size
    holder = (spot - (spot & 1)) + (source & 1)
    index = ((source >> 1) ^ meta[2]) * 2 + ((spot ^ (meta[0] >> 1)) & 1)
    return meta[1] ^ holder, index


def late_kernel(group_size, reuse, meta, turned, top_in, sum_in, *refs):
    pieces = refs[:group_size]
    out, top_ref, sum_ref, buffer, semaphores = refs[group_size:]
    place = functools.partial(fresh_place, group_size, meta)
    count = start_pages(reuse, 0, place, pieces, buffer, semaphores)
    top_ref[...] = jnp.full_like(top_ref, MASK_VALUE)
    sum_ref[...] = jnp.zeros_like(sum_ref)

    def wait_page(index):
        pltpu.make_async_copy(pieces[0].at[0], buffer.at[index], semaphores.at[index]).wait()

    fold_pages(turned, buffer, wait_page, count, top_ref, sum_ref)
    for group in range(GQ):
        first_top, last_top = top_in[group], top_ref[group]
        row_top = jnp.maximum(first_top, last_top)
        first_share, last_share = jnp.exp(first_top - row_top), jnp.exp(last_top - row_top)
        total = sum_in[group] * jnp.concatenate([first_share, first_share], axis=1)
        total += sum_ref[group] * jnp.concatenate([last_share, last_share], axis=1)
        out[:, group * HEAD_DIM : (group + 1) * HEAD_DIM] = (
            total[:, :HEAD_DIM] / total[:, HEAD_DIM:]
        ).astype(out.dtype)


def attend_late(reuse, meta, turned, top, total, pieces):
    page_count, row_count, page_rows = reuse.shape[0], turned.shape[1], pieces[0].shape[1]
    group_size = len(pieces)
    most = min(page_count, group_size * pieces[0].shape[0])
    in_smem = pl.BlockSpec(memory_space=pltpu.SMEM)
    in_vmem = pl.BlockSpec(memory_space=pltpu.VMEM)
    anywhere = pl.BlockSpec(memory_space=pl.ANY)
    work = GQ * row_count * page_rows * page_count // 2
    return pl.pallas_call(
        functools.partial(late_kernel, group_size),
        in_specs=[in_smem] * 2 + [in_vmem] * 3 + [anywhere] * group_size,
        out_specs=in_vmem,
        out_shape=jax.ShapeDtypeStruct((row_count, GQ * HEAD_DIM), jnp.bfloat16),
        scratch_shapes=[
            pltpu.VMEM(top.shape, top.dtype),
            pltpu.VMEM(total.shape, total.dtype),
            pltpu.VMEM((most, page_rows, PAIR), jnp.bfloat16),
            pltpu.SemaphoreType.DMA((most,)),
        ],
        compiler_params=pltpu.CompilerParams(vmem_limit_bytes=24 << 20),
        cost_estimate=pl.CostEstimate(
            flops=4 * work * HEAD_DIM,
            bytes_accessed=page_rows * page_count * PAIR,
            transcendentals=work,
        ),
        name="late",
    )(reuse, meta, turned, top, total, *pieces)


def on_device(parts, queries, ext_kv, page_store, prefix_hidden, kv_weight, kv_bias, reuse):
    devices = lax.axis_size("kv")
    own_index = lax.axis_index("kv")
    part_index = lax.axis_index("grp")
    row_count = queries.shape[0]
    group_size = devices // HEADS
    group_bits = group_size.bit_length() - 1
    head = own_index >> group_bits
    slice_index = own_index & (group_size - 1)
    core = own_index & 1
    side = part_index & 1
    page_count = reuse.shape[0]
    slots, page_rows = page_store.shape[0], page_store.shape[1]

    def exchange(value, bit):
        return swap(value, "kv", bit, devices)

    def between_planes(value):
        groups = [list(range(spot, devices, group_size)) for spot in range(group_size)]
        return lax.all_to_all(value, "kv", 0, 0, axis_index_groups=groups, tiled=True)

    hidden_across = swap(prefix_hidden, "grp", 1, parts)

    target = 2 * core + side
    spare = 2 * (1 - core) + side
    mine = lax.dynamic_slice_in_dim(kv_weight, target * PAIR, PAIR, 1)
    other = exchange(lax.dynamic_slice_in_dim(kv_weight, spare * PAIR, PAIR, 1), 1)
    chip_rows = jnp.where(
        core == 0,
        jnp.concatenate([mine, other], axis=0),
        jnp.concatenate([other, mine], axis=0),
    )

    def as_pages(*blocks):
        return jnp.concatenate(blocks, axis=0).reshape(-1, page_rows, PAIR)

    def stored_for(store, plane):
        part = lax.dynamic_slice_in_dim(store, plane * PAIR, PAIR, 2)
        return part.reshape(slots * page_rows, PAIR)

    order = []
    if group_size == 4:
        def to_plane(value, shift):
            step = shift * group_size
            return lax.ppermute(value, "kv", [(i, (i + step) % devices) for i in range(devices)])

        near, back = to_plane(chip_rows, 1), to_plane(chip_rows, 3)
        store_beside = exchange(page_store, 2)
        far = to_plane(near, 1)
        near_sent, own_sent, store_beside = lax.optimization_barrier(
            (near, chip_rows, store_beside)
        )
        beside_near = exchange(near_sent, 2)
        beside_own = exchange(own_sent, 2)
        back_sent, _ = lax.optimization_barrier((back, beside_near))
        beside_back = exchange(back_sent, 2)
        far_sent, hidden_mine, hidden_passed, reuse_sent, stores, _ = lax.optimization_barrier(
            (far, prefix_hidden, hidden_across, reuse, (page_store, store_beside), beside_back)
        )
        hidden_core = exchange(hidden_mine, 1)
        beside_far = exchange(far_sent, 2)
        def parts_for(shift):
            return as_pages(*[stored_for(store, (head + shift) & (HEADS - 1)) for store in stores])

        others = [
            lax.ppermute(
                parts_for(shift),
                "kv",
                [(i, (i + shift * group_size) % devices) for i in range(devices)],
            )
            for shift in (1, 3, 2)
        ]
        own_parts = parts_for(0)
        weights = [chip_rows, beside_own, near, beside_near, back, beside_back, far, beside_far]
        for shift in (0, 1, 3, 2):
            chip = (((head - shift) & (HEADS - 1)) << 1) | (slice_index >> 1)
            order += [chip, chip ^ 1]
    else:
        hidden_core, hidden_passed, reuse_sent = exchange(prefix_hidden, 1), hidden_across, reuse
        weights = [
            lax.all_gather(
                chip_rows,
                "kv",
                axis=0,
                tiled=True,
                axis_index_groups=[list(range(first, devices, 2)) for first in range(2)],
            )
        ]
    hidden_diagonal = exchange(hidden_passed, 1)
    reuse_across = swap(reuse_sent, "grp", 1, parts)
    offset = page_count * page_rows
    (ext_kv, first_row), _ = lax.optimization_barrier(
        ((ext_kv, slice_index * row_count), weights[min(2, len(weights) - 1)])
    )
    query_pos = offset + first_row + jnp.arange(row_count, dtype=jnp.int32)
    row_cos, row_sin = angle_tables(query_pos)
    raw_keys = ext_kv[:, :HEAD_DIM].astype(jnp.float32)
    own_keys = raw_keys * row_cos + jnp.roll(raw_keys, HEAD_DIM // 2, axis=1) * row_sin
    own_block = jnp.concatenate([own_keys.astype(jnp.bfloat16), ext_kv[:, HEAD_DIM:]], axis=1)

    if group_size == 4:
        own_sent, _ = lax.optimization_barrier((own_block, weights[5]))
        block_beside = as_pages(exchange(own_sent, 2))
        own_pages = as_pages(own_block)
        own_cores = [exchange(own_parts, 1), exchange(own_pages, 1)]

    def page_numbers(table):
        match = (table[:, 0] == 0)[:, None] & (
            table[:, 2][:, None] == jnp.stack([own_index, own_index ^ 1])[None, :]
        )
        return jnp.sum(
            jnp.where(match, jnp.arange(page_count, dtype=jnp.int32)[:, None], 0), axis=0
        )

    numbers = jnp.concatenate([page_numbers(reuse), page_numbers(reuse_across)])
    page_cos, page_sin = angle_tables(
        numbers[:, None] * page_rows + jnp.arange(page_rows, dtype=jnp.int32)[None, :]
    )

    bias = lax.dynamic_slice_in_dim(kv_bias, target * PAIR, PAIR, 0).astype(jnp.float32)[None, :]
    first_side = (head >> 1) ^ side
    choice = jnp.stack([first_side, first_side ^ 1] + order).astype(jnp.int32)
    messages = project(
        choice,
        (prefix_hidden, hidden_core, hidden_across, hidden_diagonal),
        weights,
        bias,
        page_cos,
        page_sin,
    )
    received = []
    for turn, message in enumerate(messages):
        routes = []
        for part in range(parts):
            for device in range(devices):
                plane, spot = device // group_size, device % group_size
                to_part = (part & ~1) | ((plane >> 1) ^ turn)
                to_spot = (spot & ~1) | (plane & 1)
                to_head = 2 * (spot & 1) + (part & 1)
                routes.append(
                    (part * devices + device, to_part * devices + to_head * group_size + to_spot)
                )
        received.append(lax.ppermute(message, ("grp", "kv"), routes))
    meta = jnp.stack([head, slice_index, side]).astype(jnp.int32)
    bits = []
    while 1 << len(bits) < group_size:
        bits.insert(0, 1 << len(bits))

    def spread(own, first):
        pieces = {0: own, bits[0]: first}
        for bit in bits[1:]:
            pieces.update({known ^ bit: exchange(value, bit) for known, value in pieces.items()})
        return [pieces[relative] for relative in range(group_size)]

    if group_size == 4:
        others, block_beside = lax.optimization_barrier(
            ((others, block_beside), received)
        )[0]
        pieces = [own_parts, *others, own_pages, block_beside]
        pieces += [
            own_cores[0],
            *[exchange(piece, 1) for piece in others],
            own_cores[1],
            exchange(block_beside, 1),
        ]
        place = place_apart
        extension_at = lambda relative: ((relative & 1) * 6 + 4 + (relative >> 1), 0)
    else:
        per_head = page_store.reshape(slots, page_rows, HEADS, PAIR).transpose(2, 0, 1, 3)
        arrived = between_planes(per_head.reshape(HEADS * slots, page_rows, PAIR))
        gathered = as_pages(arrived.reshape(-1, PAIR), own_block)
        pieces = spread(gathered, exchange(gathered, bits[0]))
        place = functools.partial(place_spread, group_size)
        extension_at = lambda relative: (relative, HEADS * slots)
    turned, top, total = attend_early(
        place, extension_at, group_size, slots, reuse, meta, queries, row_cos, row_sin, pieces
    )
    late_own = jnp.concatenate(received, axis=0)
    late_first = exchange(late_own, bits[0])
    late_first, turned = lax.optimization_barrier((late_first, turned))
    late_pieces = spread(late_own, late_first)
    return attend_late(reuse, meta, turned, top, total, late_pieces)


def solution(mesh):
    placed = (
        P(("grp", "kv"), None),
        P(("grp", "kv"), None),
        P(("grp", "kv"), None, None),
        P(("grp", "kv"), None, None),
        P("kv", None),
        P(),
        P("grp", None),
    )
    return jax.shard_map(
        functools.partial(on_device, mesh.shape["grp"]),
        mesh=mesh,
        in_specs=placed,
        out_specs=P(("grp", "kv"), None),
        check_vma=False,
    )
```
